32 devices in a mesh: pole: 2 (over x), row: 8 (over z, y), col: 2 (over core).
Axes of the slice: x: 2, y: 2, z: 4, core: 2. Of those that a mesh axis runs over, the one named last changes fastest.
Arguments:
- panel: bfloat16 [4, 8, 2, 512, 128], P(('pole', 'col'), None, None, 'row'), parts along dimension 0, may hold values from -6 to 6
- tiles: bfloat16 [352, 2, 512, 512], P(('pole', 'row', 'col')), parts along dimension 0, may hold values from -0.078125 to 0.078125
- tile_slot: int32 [352], P(('pole', 'row', 'col')), parts along dimension 0, may hold values from 0 to 1
- tile_col: int32 [352], P(('pole', 'row', 'col')), parts along dimension 0, may hold values from 0 to 7
- pole_weight: float32 [4], P('pole'), parts along dimension 0, may hold values from -4 to 4
- box_orbitals: int32 [64, 256], P(('pole', 'row', 'col')), parts along dimension 0, may hold values from 0 to 8191, as said below
- box_basis: bfloat16 [64, 256, 512], P(('pole', 'row', 'col')), parts along dimension 0, may hold values from -0.375 to 0.375
- supernode_basis: bfloat16 [64, 128, 512], P(('pole', 'row', 'col')), parts along dimension 0, may hold values from -0.5 to 0.5
Outputs:
- inverse_column: float32 [32, 2, 512, 128], P(('pole', 'row'), None, 'col'), parts along dimension 0
- density: float32 [64, 512], P(('pole', 'row', 'col')), parts along dimension 0
The draws below stay inside these ranges and needn't reach their ends.
There are 2 independent parts, one for each index of `pole`. The reference program is written for one: setup_inputs(seed, part) draws one part's arguments, and reference() takes and returns one part's arrays. A program takes and returns all parts, laid end to end along the dimension named above; each array names one. Nothing has to cross between parts.
Inputs may be any that keep to these rules, and one draw needn't show every extreme that they name: `box_orbitals`: let a row g be held by device r * 2 + c where r = (g // 512) // 2 and c = (g % 512) // (512 // 2). The 2 boxes of one device take at most 64 rows (counted with repeats) held by any one device, and exactly 64 from some device.
All inputs are finite; a program needn't handle non-finite values.
Results may differ from the reference program's by a relative error of at most 0.0029.
Values may be sent and summed in bfloat16 or wider, within the bound.
No kernel may reach another device: no remote copies, remote signals or barrier semaphores. Data moves between devices by JAX's collectives and lax.ppermute only.
A program may use at most 64 MiB of HBM per device.

```python
import jax
import jax.numpy as jnp
from jax import lax

B = 512
S = 128
PTS = 512
ORB_BOX = 256
NJP = 8
BR_DEV = 2
TILE_DEV = 11
BOX_DEV = 2
TILES = 176
NBOX = 32
N_ROW = 8
N_COL = 2


def draw_box_orbitals(key, part):
    devices = N_ROW * N_COL
    per_device = BOX_DEV * ORB_BOX
    capacity = 2 * per_device // devices
    half_rows = B // N_COL
    local_total = BR_DEV * half_rows

    def one_device(device_index):
        device_key = jax.random.fold_in(key, device_index + 7919)
        subkeys = jax.random.split(device_key, 4)
        forced = jax.random.randint(subkeys[0], (), 0, devices).astype(jnp.int32)
        others = jnp.arange((devices - 1) * capacity, dtype=jnp.int32) // capacity
        others = others + (others >= forced).astype(jnp.int32)
        others = jax.random.permutation(subkeys[1], others)[:per_device - capacity]
        sources = jnp.concatenate([jnp.full((capacity,), 1, jnp.int32) * forced, others])
        sources = jax.random.permutation(subkeys[2], sources)
        local_pick = jax.random.randint(subkeys[3], (per_device,), 0, local_total).astype(jnp.int32)
        block_row = sources // N_COL * BR_DEV + local_pick // half_rows
        return block_row * B + sources % N_COL * half_rows + local_pick % half_rows
    result = jax.vmap(one_device)(jnp.arange(devices, dtype=jnp.int32))
    return result.reshape(devices * BOX_DEV, ORB_BOX).astype(jnp.int32)


def touch_ends(array, key, smallest, largest):
    longest = array.shape.index(max(array.shape))
    spots = []
    for shift in (0, 1):
        where = [jax.random.randint(jax.random.fold_in(key, axis), (), 0, length) for axis, length in enumerate(array.shape)]
        where[longest] = (where[longest] + shift) % array.shape[longest]
        spots.append(tuple(where))
    return array.at[spots[0]].set(smallest).at[spots[1]].set(largest)


def level_of(own_key, shape, cuts, low, largest):
    loudness = 1.0
    for axis_at, blocks in cuts:
        steps = jax.random.uniform(jax.random.fold_in(jax.random.fold_in(own_key, 6), axis_at), (blocks,), jnp.float32, low / len(cuts), largest / len(cuts))
        loudness = loudness * jnp.repeat(jnp.exp(steps), shape[axis_at] // blocks).reshape((-1,) + (1,) * (len(shape) - 1 - axis_at))
    return loudness


def normal_values(stream_key, shape, spread, bound, shards=(), kind=jnp.bfloat16):
    array = spread * jax.random.normal(stream_key, shape, jnp.float32)
    if shards:
        array = array * level_of(stream_key, shape, shards, -0.22, 0.18)
    return jnp.clip(array, -bound, bound).astype(kind)


def setup_inputs(seed: int = 0, part: int = 0) -> dict:
    seeds = jax.random.split(jax.random.key(seed), 9)
    part_splits = jax.random.split(jax.random.fold_in(seeds[8], part), 9)
    panel = normal_values(part_splits[0], (N_COL, NJP, 2, B, S), 1.0, 6.0, ((0, 2), (3, 8)))
    tiles = normal_values(part_splits[1], (TILES, 2, B, B), (2 * B * TILE_DEV // BR_DEV) ** -0.5, 0.078125, ((0, 16),))
    tile_slot = touch_ends(jax.random.randint(part_splits[2], (TILES,), 0, BR_DEV), jax.random.fold_in(part_splits[2], 1), 0, BR_DEV - 1).astype(jnp.int32)
    tile_col = touch_ends(jax.random.randint(part_splits[3], (TILES,), 0, NJP), jax.random.fold_in(part_splits[3], 1), 0, NJP - 1).astype(jnp.int32)
    pole_weight = normal_values(part_splits[4], (2,), 1.0, 4.0, (), jnp.float32)
    box_orbitals = draw_box_orbitals(jax.random.fold_in(jax.random.fold_in(seeds[8], part), 71), part)
    box_basis = normal_values(part_splits[6], (NBOX, ORB_BOX, PTS), ORB_BOX ** -0.5, 0.375, ((0, 16),))
    supernode_basis = normal_values(part_splits[7], (NBOX, S, PTS), S ** -0.5, 0.5, ((0, 16),))
    return {"panel": panel, "tiles": tiles, "tile_slot": tile_slot, "tile_col": tile_col, "pole_weight": pole_weight, "box_orbitals": box_orbitals, "box_basis": box_basis, "supernode_basis": supernode_basis}


def reference(panel, tiles, tile_slot, tile_col, pole_weight, box_orbitals, box_basis, supernode_basis):
    tile_total = tiles.shape[0]

    def add_tile(column, inputs):
        tile_block, slot_row, block_col, tile_index = inputs
        device = tile_index // TILE_DEV
        block_row = ((device // N_COL) * BR_DEV + slot_row).astype(jnp.int32)
        factor = panel[device % N_COL, block_col].astype(jnp.float32)
        tile_wide = tile_block.astype(jnp.float32)
        real_part = jnp.dot(tile_wide[0], factor[0]) - jnp.dot(tile_wide[1], factor[1])
        imag_part = jnp.dot(tile_wide[0], factor[1]) + jnp.dot(tile_wide[1], factor[0])
        update = jnp.stack([real_part, imag_part], axis=0)
        column = column.at[block_row].add(update)
        return column, None

    start_column = jnp.zeros((BR_DEV * N_ROW, 2, B, S), jnp.float32)
    indices = jnp.arange(tile_total, dtype=jnp.int32)
    column, _ = lax.scan(add_tile, start_column, (tiles, tile_slot, tile_col, indices))
    inverse_column = -column
    density_rows = (pole_weight[0] * inverse_column[:, 1] + pole_weight[1] * inverse_column[:, 0]).astype(jnp.bfloat16)
    density_rows = density_rows.reshape(-1, S)
    picked = jnp.take(density_rows, box_orbitals, axis=0)
    projected = jnp.einsum("nas,nap->nsp", picked.astype(jnp.float32), box_basis.astype(jnp.float32))
    density = jnp.sum(supernode_basis.astype(jnp.float32) * projected, axis=1)
    return inverse_column, density
```

```python
import functools

import jax
import jax.numpy as jnp
from jax import lax
from jax.experimental import pallas as pl
from jax.experimental.pallas import tpu as pltpu
from jax.sharding import PartitionSpec as P

BR_DEV = 2
LANES = 128
F32 = jnp.float32
BF16 = jnp.bfloat16
VMEM_LIMIT = 48 * 1024 * 1024


def ring_order(n):
    if n <= 8 and n % 2 == 0:
        return list(range(0, n, 2)) + list(range(n - 1, 0, -2))
    return list(range(n))


def full_spec(shape):
    zeros = (0,) * len(shape)
    return pl.BlockSpec(shape, lambda *_: zeros)


def place(factor, first, count):
    depth = factor.shape[1]
    reps = LANES // depth
    row = lax.broadcasted_iota(jnp.int32, (LANES, factor.shape[2]), 0)
    inside = (row // depth) == first
    spread = [
        jnp.where(inside, jnp.concatenate([factor[p].astype(F32)] * reps, axis=0), 0.0)
        for p in range(2)
    ]
    upper = jnp.concatenate([spread[0], spread[1]], axis=1)
    lower = jnp.concatenate([-spread[1], spread[0]], axis=1)
    return jnp.concatenate([upper, lower], axis=0).astype(BF16)


def accumulate(meta, where, factors, blocks, acc, weights, tile_count, reps):
    step = pl.program_id(0)
    for s, parts in enumerate(factors):
        done = 0
        for part in parts:
            for j in range(part.shape[0]):
                @pl.when(step == 0)
                def _(part=part, j=j, s=s, at=done + j):
                    weights[at, s * 2 * LANES:(s + 1) * 2 * LANES, :] = place(
                        part[j], meta[where[s]] % reps, reps
                    )
            done += part.shape[0]
    slot = meta[step]
    block = meta[tile_count + step]
    left = jnp.concatenate([b[0, p] for b in blocks for p in range(2)], axis=1)
    acc[slot] += jnp.dot(left, weights[block], preferred_element_type=F32)


def hop_first(meta, own, tile, out, weights, *, tile_count, where, reps):
    @pl.when(pl.program_id(0) == 0)
    def _():
        out[...] = jnp.zeros_like(out)
    accumulate(meta, where, [[own]], [tile], out, weights, tile_count, reps)


def hop_middle(meta, from_left, from_right, tile_a, tile_b, start, out, weights, *, tile_count, where, reps):
    @pl.when(pl.program_id(0) == 0)
    def _():
        out[...] = start[...]
    accumulate(meta, where, [[from_left], [from_right]], [tile_a, tile_b], out, weights, tile_count, reps)


def hop_last(meta, pole_weight, low, high, tile, start, dens, mine, other, acc, weights, *, tile_count, where, reps, col_at):
    step = pl.program_id(0)

    @pl.when(step == 0)
    def _():
        acc[...] = start[...]
    accumulate(meta, where, [[low, high]], [tile], acc, weights, tile_count, reps)

    @pl.when(step == tile_count - 1)
    def _():
        col = meta[col_at]
        half = mine.shape[2]
        width = mine.shape[3]
        for slot in range(acc.shape[0]):
            real = -acc[slot, :, :width]
            imag = -acc[slot, :, width:]
            dens[slot] = pole_weight[0] * imag + pole_weight[1] * real
            for p in range(2):
                cols = slice(p * width, (p + 1) * width)
                mine[slot, p] = -acc[slot, pl.ds(pl.multiple_of(col * half, half), half), cols]
                other[slot, p] = -acc[slot, pl.ds(pl.multiple_of((1 - col) * half, half), half), cols]


def basis_kernel(wanted_row, wanted_col, basis, out, *, rows_chip, slots):
    total = wanted_row.shape[1]
    src_row = wanted_row[...] // rows_chip
    src_col = wanted_col[...] // rows_chip
    at_col = lax.broadcasted_iota(jnp.int32, (total, total), 0)
    at_row = lax.broadcasted_iota(jnp.int32, (total, total), 1)
    before = ((src_col == src_row) & (at_col < at_row)).astype(F32)
    rank = jnp.sum(before, axis=0, keepdims=True).astype(jnp.int32)
    slot = src_row * slots + rank
    boxes, orbitals, _ = basis.shape
    arrive = out.shape[1]
    for n in range(boxes):
        index = lax.broadcasted_iota(jnp.int32, (arrive, orbitals), 0)
        pick = (index == slot[:, n * orbitals:(n + 1) * orbitals]).astype(F32).astype(BF16)
        out[n] = jnp.dot(pick, basis[n], preferred_element_type=F32).astype(BF16)


def pick_kernel(me, wanted, out, *, rows_chip, slots):
    dests, total = wanted.shape
    asked = wanted[...]
    here = (asked // rows_chip) == me[0]
    local = (asked % rows_chip).astype(F32)
    at_col = lax.broadcasted_iota(jnp.int32, (total, total), 0)
    at_row = lax.broadcasted_iota(jnp.int32, (total, total), 1)
    earlier = (at_col < at_row).astype(F32).astype(BF16)
    rank = jnp.dot(here.astype(F32).astype(BF16), earlier, preferred_element_type=F32).astype(jnp.int32)
    rank = jnp.where(here, rank, -1)
    index = lax.broadcasted_iota(jnp.int32, (slots, total), 0)
    lane = lax.broadcasted_iota(jnp.int32, (slots, rows_chip), 1)
    for d in range(dests):
        chosen = jnp.where(index == rank[d:d + 1], local[d:d + 1], 0.0)
        row = jnp.sum(chosen, axis=1, keepdims=True).astype(jnp.int32)
        out[d * slots:(d + 1) * slots, :] = (lane == row).astype(F32).astype(BF16)


def select_kernel(pick, mine, theirs, out):
    rows = pick.shape[1]
    total = (mine[...] + theirs[...]).reshape(rows, mine.shape[2]).astype(BF16)
    out[...] = jnp.dot(pick[...], total, preferred_element_type=F32).astype(BF16)


def density_kernel(arrived, basis, supernode, out):
    for n in range(basis.shape[0]):
        projected = lax.dot_general(
            arrived[...], basis[n], (((0,), (0,)), ((), ())), preferred_element_type=F32
        )
        out[n:n + 1, :] = jnp.sum(supernode[n].astype(F32) * projected, axis=0, keepdims=True)


def local(n_row, panel, tiles, tile_slot, tile_col, pole_weight, box_orbitals, box_basis, supernode_basis):
    order = ring_order(n_row)
    half_ring = n_row // 2
    to_right = [(order[i], order[(i + 1) % n_row]) for i in range(n_row)]
    to_left = [(order[(i + 1) % n_row], order[i]) for i in range(n_row)]
    row = lax.axis_index("row").astype(jnp.int32)
    col = lax.axis_index("col").astype(jnp.int32)

    own = panel[0]
    blocks, parts, depth, width = own.shape
    tile_count, _, order_b, _ = tiles.shape
    reps = LANES // depth
    boxes, orbitals = box_orbitals.shape
    wanted_total = boxes * orbitals
    rows_chip = BR_DEV * order_b
    slots = 2 * wanted_total // n_row
    half = order_b // 2

    table = jnp.asarray(order, jnp.int32)
    position = jnp.sum(jnp.where(table == row, jnp.arange(n_row, dtype=jnp.int32), 0))
    offsets = [0]
    for h in range(1, half_ring):
        offsets += [-h, h]
    offsets.append(half_ring)
    at = (position + jnp.asarray(offsets, jnp.int32)) % n_row
    shard_rows = jnp.sum(jnp.where(at[:, None] == jnp.arange(n_row)[None], table[None], 0), axis=1)
    meta = jnp.concatenate([tile_slot, tile_col, shard_rows.astype(jnp.int32), col[None]])
    base = 2 * tile_count
    col_at = base + len(offsets)

    factor_spec = full_spec(own.shape)
    acc_shape = (BR_DEV, order_b, 2 * width)

    def tile_spec(where):
        return pl.BlockSpec(
            (1, 2, order_b, LANES), lambda t, meta: (t, 0, 0, meta[where] // reps)
        )

    def call(body, in_specs, out_specs, out_shape, scratch, shards, aliases=None):
        return pl.pallas_call(
            body,
            grid_spec=pltpu.PrefetchScalarGridSpec(
                num_scalar_prefetch=1,
                grid=(tile_count,),
                in_specs=in_specs,
                out_specs=out_specs,
                scratch_shapes=scratch,
            ),
            out_shape=out_shape,
            compiler_params=pltpu.CompilerParams(
                dimension_semantics=("arbitrary",), vmem_limit_bytes=VMEM_LIMIT
            ),
            cost_estimate=pl.CostEstimate(
                flops=shards * tile_count * order_b * 256 * 256 * 4,
                bytes_accessed=shards * tile_count * order_b * 256 * 2,
                transcendentals=0,
            ),
        )

    acc_out = jax.ShapeDtypeStruct(acc_shape, F32)

    wanted = box_orbitals.reshape(1, wanted_total)
    asked = wanted
    left, right = own, own
    acc = None
    distance = 1
    for h in range(1, half_ring + 1):
        if h < half_ring:
            next_left = lax.ppermute(left, "row", to_right)
            next_right = lax.ppermute(right, "row", to_left)
        else:
            cut = blocks // 2
            next_left = lax.ppermute(left[:cut], "row", to_right)
            next_right = lax.ppermute(right[cut:], "row", to_left)
        if distance < n_row:
            got = lax.ppermute(asked, "row", [(i, i ^ distance) for i in range(n_row)])
            low = (row // distance) % 2 == 0
            asked = jnp.concatenate(
                [jnp.where(low, asked, got), jnp.where(low, got, asked)], axis=0
            )
            distance *= 2
        if h == 1:
            acc = call(
                functools.partial(hop_first, tile_count=tile_count, where=[base], reps=reps),
                [factor_spec, tile_spec(base)],
                full_spec(acc_shape),
                acc_out,
                [pltpu.VMEM((blocks, 2 * LANES, 2 * width), BF16)],
                1,
            )(meta, own, tiles)
        else:
            at_h = [base + 2 * h - 3, base + 2 * h - 2]
            acc = call(
                functools.partial(hop_middle, tile_count=tile_count, where=at_h, reps=reps),
                [factor_spec, factor_spec, tile_spec(at_h[0]), tile_spec(at_h[1]), full_spec(acc_shape)],
                full_spec(acc_shape),
                acc_out,
                [pltpu.VMEM((blocks, 4 * LANES, 2 * width), BF16)],
                2,
            )(meta, left, right, tiles, tiles, acc)
        left, right = next_left, next_right

    half_shape = (BR_DEV, 2, half, width)
    dens_shape = (BR_DEV, order_b, width)
    last = base + len(offsets) - 1
    dens, mine, other = call(
        functools.partial(hop_last, tile_count=tile_count, where=[last], reps=reps, col_at=col_at),
        [
            pl.BlockSpec(memory_space=pltpu.SMEM),
            full_spec(left.shape),
            full_spec(right.shape),
            tile_spec(last),
            full_spec(acc_shape),
        ],
        [full_spec(dens_shape), full_spec(half_shape), full_spec(half_shape)],
        [
            jax.ShapeDtypeStruct(dens_shape, F32),
            jax.ShapeDtypeStruct(half_shape, F32),
            jax.ShapeDtypeStruct(half_shape, F32),
        ],
        [pltpu.VMEM(acc_shape, F32), pltpu.VMEM((blocks, 2 * LANES, 2 * width), BF16)],
        1,
    )(meta, pole_weight, left, right, tiles, acc)

    arrive = n_row * slots
    params = pltpu.CompilerParams(vmem_limit_bytes=VMEM_LIMIT)
    basis_here = pl.pallas_call(
        functools.partial(basis_kernel, rows_chip=rows_chip, slots=slots),
        out_shape=jax.ShapeDtypeStruct((boxes, arrive, box_basis.shape[2]), BF16),
        compiler_params=params,
        cost_estimate=pl.CostEstimate(
            flops=2 * arrive * wanted_total * box_basis.shape[2], bytes_accessed=2 ** 21, transcendentals=0
        ),
    )(wanted, box_orbitals.reshape(wanted_total, 1), box_basis)
    pick = pl.pallas_call(
        functools.partial(pick_kernel, rows_chip=rows_chip, slots=slots),
        in_specs=[pl.BlockSpec(memory_space=pltpu.SMEM), pl.BlockSpec(memory_space=pltpu.VMEM)],
        out_shape=jax.ShapeDtypeStruct((arrive, rows_chip), BF16),
        compiler_params=params,
        cost_estimate=pl.CostEstimate(
            flops=2 * arrive * wanted_total * 512, bytes_accessed=2 ** 21, transcendentals=0
        ),
    )(row[None], asked)

    swap = [(0, 1), (1, 0)]
    dens_other = lax.ppermute(dens, "col", swap)
    inverse_other = lax.ppermute(other, "col", swap)
    send = pl.pallas_call(
        select_kernel,
        out_shape=jax.ShapeDtypeStruct((arrive, width), BF16),
        compiler_params=params,
    )(pick, dens, dens_other)
    arrived = lax.all_to_all(send, "row", 0, 0, tiled=True)
    density = pl.pallas_call(
        density_kernel,
        out_shape=jax.ShapeDtypeStruct((boxes, box_basis.shape[2]), F32),
        compiler_params=params,
    )(arrived, basis_here, supernode_basis)
    return mine + inverse_other, density


def solution(mesh):
    return jax.shard_map(
        functools.partial(local, mesh.shape["row"]),
        mesh=mesh,
        in_specs=(
            P(("pole", "col"), None, None, "row", None),
            P(("pole", "row", "col"), None, None, None),
            P(("pole", "row", "col")),
            P(("pole", "row", "col")),
            P("pole"),
            P(("pole", "row", "col"), None),
            P(("pole", "row", "col"), None, None),
            P(("pole", "row", "col"), None, None),
        ),
        out_specs=(P(("pole", "row"), None, "col", None), P(("pole", "row", "col"), None)),
        check_vma=False,
    )
```

```python
import functools

import jax
import jax.numpy as jnp
from jax import lax
from jax.experimental import pallas as pl
from jax.experimental.pallas import tpu as pltpu
from jax.sharding import PartitionSpec as P

BR_DEV = 2
LANES = 128
F32 = jnp.float32
BF16 = jnp.bfloat16
VMEM_LIMIT = 16 * 1024 * 1024


def ring_order(n):
    if n <= 8 and n % 2 == 0:
        return list(range(0, n, 2)) + list(range(n - 1, 0, -2))
    return list(range(n))


def shard_row(n, hop):
    row = lax.axis_index("row")
    if ring_order(n) == list(range(n)):
        return lax.rem(row + hop + n, n)
    at = jnp.where(row % 2 == 0, row // 2, n - 1 - row // 2)
    at = lax.rem(at + hop + n, n)
    return jnp.where(at < n // 2, 2 * at, 2 * (n - 1 - at) + 1)


def place(factor, first):
    depth = factor.shape[1]
    reps = LANES // depth
    row = lax.broadcasted_iota(jnp.int32, (LANES, factor.shape[2]), 0)
    inside = (row // depth) == first
    spread = [
        jnp.where(inside, jnp.concatenate([factor[p].astype(F32)] * reps, axis=0), 0.0)
        for p in range(2)
    ]
    upper = jnp.concatenate([spread[0], spread[1]], axis=1)
    lower = jnp.concatenate([-spread[1], spread[0]], axis=1)
    return jnp.concatenate([upper, lower], axis=0).astype(BF16)


def accumulate(slots, cols, tiles, shards, acc, weights):
    starts = []
    for s, (row, parts) in enumerate(shards):
        reps = LANES // parts[0].shape[2]
        starts.append(pl.multiple_of(row // reps * LANES, LANES))
        at = 0
        for part in parts:
            for j in range(part.shape[0]):
                weights[at, s * 2 * LANES:(s + 1) * 2 * LANES, :] = place(part[j], row % reps)
                at += 1
    for t in range(tiles.shape[0]):
        left = jnp.concatenate(
            [tiles[t, p, :, pl.ds(start, LANES)] for start in starts for p in range(2)], axis=1
        )
        acc[slots[t]] += jnp.dot(left, weights[cols[t]], preferred_element_type=F32)


def hop_first(slots, cols, own, tiles, out, weights, *, n):
    out[...] = jnp.zeros_like(out)
    accumulate(slots, cols, tiles, [(shard_row(n, 0), [own])], out, weights)


def hop_middle(slots, cols, from_left, from_right, tiles, start, out, weights, *, n, hop):
    out[...] = start[...]
    shards = [(shard_row(n, -hop), [from_left]), (shard_row(n, hop), [from_right])]
    accumulate(slots, cols, tiles, shards, out, weights)


def hop_last(slots, cols, pole_weight, low, high, tiles, start, dens, mine, other, acc, weights, *, n):
    acc[...] = start[...]
    accumulate(slots, cols, tiles, [(shard_row(n, n // 2), [low, high])], acc, weights)
    col = lax.axis_index("col")
    half = mine.shape[2]
    width = mine.shape[3]
    for slot in range(acc.shape[0]):
        real = -acc[slot, :, :width]
        imag = -acc[slot, :, width:]
        dens[slot] = pole_weight[0] * imag + pole_weight[1] * real
        for p in range(2):
            cut = slice(p * width, (p + 1) * width)
            mine[slot, p] = -acc[slot, pl.ds(pl.multiple_of(col * half, half), half), cut]
            other[slot, p] = -acc[slot, pl.ds(pl.multiple_of((1 - col) * half, half), half), cut]


def basis_kernel(wanted_row, wanted_col, basis, out, *, rows_chip, slots):
    total = wanted_row.shape[1]
    src_row = wanted_row[...] // rows_chip
    src_col = wanted_col[...] // rows_chip
    at_col = lax.broadcasted_iota(jnp.int32, (total, total), 0)
    at_row = lax.broadcasted_iota(jnp.int32, (total, total), 1)
    before = ((src_col == src_row) & (at_col < at_row)).astype(F32)
    rank = jnp.sum(before, axis=0, keepdims=True).astype(jnp.int32)
    slot = src_row * slots + rank
    boxes, orbitals, _ = basis.shape
    arrive = out.shape[1]
    for n in range(boxes):
        index = lax.broadcasted_iota(jnp.int32, (arrive, orbitals), 0)
        pick = (index == slot[:, n * orbitals:(n + 1) * orbitals]).astype(F32).astype(BF16)
        out[n] = jnp.dot(pick, basis[n], preferred_element_type=F32).astype(BF16)


def pick_kernel(wanted, out, *, rows_chip, slots):
    dests, total = wanted.shape
    asked = wanted[...]
    here = (asked // rows_chip) == lax.axis_index("row")
    local = (asked % rows_chip).astype(F32)
    at_col = lax.broadcasted_iota(jnp.int32, (total, total), 0)
    at_row = lax.broadcasted_iota(jnp.int32, (total, total), 1)
    earlier = (at_col < at_row).astype(F32).astype(BF16)
    rank = jnp.dot(here.astype(F32).astype(BF16), earlier, preferred_element_type=F32).astype(jnp.int32)
    rank = jnp.where(here, rank, -1)
    index = lax.broadcasted_iota(jnp.int32, (slots, total), 0)
    lane = lax.broadcasted_iota(jnp.int32, (slots, rows_chip), 1)
    for d in range(dests):
        chosen = jnp.where(index == rank[d:d + 1], local[d:d + 1], 0.0)
        row = jnp.sum(chosen, axis=1, keepdims=True).astype(jnp.int32)
        out[d * slots:(d + 1) * slots, :] = (lane == row).astype(F32).astype(BF16)


def select_kernel(pick, mine, theirs, out):
    rows = pick.shape[1]
    total = (mine[...] + theirs[...]).reshape(rows, mine.shape[2]).astype(BF16)
    out[...] = jnp.dot(pick[...], total, preferred_element_type=F32).astype(BF16)


def density_kernel(arrived, basis, supernode, out):
    for n in range(basis.shape[0]):
        projected = lax.dot_general(
            arrived[...], basis[n], (((0,), (0,)), ((), ())), preferred_element_type=F32
        )
        out[n:n + 1, :] = jnp.sum(supernode[n].astype(F32) * projected, axis=0, keepdims=True)


def local(n_row, panel, tiles, tile_slot, tile_col, pole_weight, box_orbitals, box_basis, supernode_basis):
    order = ring_order(n_row)
    half_ring = n_row // 2
    to_right = [(order[i], order[(i + 1) % n_row]) for i in range(n_row)]
    to_left = [(order[(i + 1) % n_row], order[i]) for i in range(n_row)]
    row = lax.axis_index("row").astype(jnp.int32)

    own = panel[0]
    blocks, parts, depth, width = own.shape
    tile_count, _, order_b, _ = tiles.shape
    boxes, orbitals = box_orbitals.shape
    wanted_total = boxes * orbitals
    rows_chip = BR_DEV * order_b
    slots = 2 * wanted_total // n_row
    half = order_b // 2
    acc_shape = (BR_DEV, order_b, 2 * width)
    acc_out = jax.ShapeDtypeStruct(acc_shape, F32)
    in_vmem = pl.BlockSpec(memory_space=pltpu.VMEM)
    in_smem = pl.BlockSpec(memory_space=pltpu.SMEM)
    params = pltpu.CompilerParams(vmem_limit_bytes=VMEM_LIMIT)

    def call(body, n_smem, n_vmem, out_shape, scratch, shards):
        return pl.pallas_call(
            body,
            in_specs=[in_smem] * n_smem + [in_vmem] * n_vmem,
            out_shape=out_shape,
            scratch_shapes=scratch + [pltpu.VMEM((blocks, shards * 2 * LANES, 2 * width), BF16)],
            compiler_params=params,
            cost_estimate=pl.CostEstimate(
                flops=shards * tile_count * order_b * 256 * 256 * 8,
                bytes_accessed=shards * tile_count * order_b * 256 * 2,
                transcendentals=0,
            ),
        )

    wanted = box_orbitals.reshape(1, wanted_total)
    asked = wanted
    left, right = own, own
    acc = None
    pick = None
    arrive = n_row * slots
    distance = 1
    for h in range(1, half_ring + 1):
        if h < half_ring:
            next_left = lax.ppermute(left, "row", to_right)
            next_right = lax.ppermute(right, "row", to_left)
        else:
            cut = blocks // 2
            next_left = lax.ppermute(left[:cut], "row", to_right)
            next_right = lax.ppermute(right[cut:], "row", to_left)
        if distance < n_row:
            got = lax.ppermute(asked, "row", [(i, i ^ distance) for i in range(n_row)])
            low = (row // distance) % 2 == 0
            asked = jnp.concatenate(
                [jnp.where(low, asked, got), jnp.where(low, got, asked)], axis=0
            )
            distance *= 2
        elif pick is None:
            pick = pl.pallas_call(
                functools.partial(pick_kernel, rows_chip=rows_chip, slots=slots),
                out_shape=jax.ShapeDtypeStruct((arrive, rows_chip), BF16),
                compiler_params=params,
                cost_estimate=pl.CostEstimate(
                    flops=2 * arrive * wanted_total * 512, bytes_accessed=2 ** 21, transcendentals=0
                ),
            )(asked)
            acc, pick = lax.optimization_barrier((acc, pick))
        if h == 1:
            acc = call(functools.partial(hop_first, n=n_row), 2, 2, acc_out, [], 1)(
                tile_slot, tile_col, own, tiles
            )
        else:
            acc, asked = lax.optimization_barrier((acc, asked))
            acc = call(functools.partial(hop_middle, n=n_row, hop=h - 1), 2, 4, acc_out, [], 2)(
                tile_slot, tile_col, left, right, tiles, acc
            )
        left, right = next_left, next_right

    half_shape = (BR_DEV, 2, half, width)
    dens_shape = (BR_DEV, order_b, width)
    dens, mine, other = call(
        functools.partial(hop_last, n=n_row),
        3,
        4,
        [
            jax.ShapeDtypeStruct(dens_shape, F32),
            jax.ShapeDtypeStruct(half_shape, F32),
            jax.ShapeDtypeStruct(half_shape, F32),
        ],
        [pltpu.VMEM(acc_shape, F32)],
        1,
    )(tile_slot, tile_col, pole_weight, left, right, tiles, acc)

    basis_here = pl.pallas_call(
        functools.partial(basis_kernel, rows_chip=rows_chip, slots=slots),
        out_shape=jax.ShapeDtypeStruct((boxes, arrive, box_basis.shape[2]), BF16),
        compiler_params=params,
        cost_estimate=pl.CostEstimate(
            flops=2 * arrive * wanted_total * box_basis.shape[2], bytes_accessed=2 ** 21, transcendentals=0
        ),
    )(wanted, box_orbitals.reshape(wanted_total, 1), box_basis)
    swap = [(0, 1), (1, 0)]
    dens_other = lax.ppermute(dens, "col", swap)
    inverse_other = lax.ppermute(other, "col", swap)
    send = pl.pallas_call(
        select_kernel,
        out_shape=jax.ShapeDtypeStruct((arrive, width), BF16),
        compiler_params=params,
    )(pick, dens, dens_other)
    arrived = lax.all_to_all(send, "row", 0, 0, tiled=True)
    density = pl.pallas_call(
        density_kernel,
        out_shape=jax.ShapeDtypeStruct((boxes, box_basis.shape[2]), F32),
        compiler_params=params,
    )(arrived, basis_here, supernode_basis)
    return mine + inverse_other, density


def solution(mesh):
    return jax.shard_map(
        functools.partial(local, mesh.shape["row"]),
        mesh=mesh,
        in_specs=(
            P(("pole", "col"), None, None, "row", None),
            P(("pole", "row", "col"), None, None, None),
            P(("pole", "row", "col")),
            P(("pole", "row", "col")),
            P("pole"),
            P(("pole", "row", "col"), None),
            P(("pole", "row", "col"), None, None),
            P(("pole", "row", "col"), None, None),
        ),
        out_specs=(P(("pole", "row"), None, "col", None), P(("pole", "row", "col"), None)),
        check_vma=False,
    )
```

```python
import functools

import jax
import jax.numpy as jnp
from jax import lax
from jax.experimental import pallas as pl
from jax.experimental.pallas import tpu as pltpu
from jax.sharding import PartitionSpec as P

BR_DEV = 2
LANES = 128
F32 = jnp.float32
BF16 = jnp.bfloat16
VMEM_LIMIT = 8 * 1024 * 1024


def ring_order(n):
    if n <= 8 and n % 2 == 0:
        return list(range(0, n, 2)) + list(range(n - 1, 0, -2))
    return list(range(n))


def shard_row(n, hop):
    row = lax.axis_index("row")
    if ring_order(n) == list(range(n)):
        return lax.rem(row + hop + n, n)
    at = jnp.where(row % 2 == 0, row // 2, n - 1 - row // 2)
    at = lax.rem(at + hop + n, n)
    return jnp.where(at < n // 2, 2 * at, 2 * (n - 1 - at) + 1)


def digits(rows):
    boxes, orbitals = rows.shape
    pieces = [rows[n:n + 1, c:c + LANES] for n in range(boxes) for c in range(0, orbitals, LANES)]
    lines = [piece // 256 for piece in pieces] + [piece % 256 for piece in pieces]
    pad = -len(lines) % 16
    lines.append(jnp.zeros((pad, LANES), jnp.int32))
    return jnp.concatenate(lines, axis=0).astype(F32).astype(BF16)


def undigits(lines, total):
    count = total // LANES
    lines = lines.astype(F32)
    whole = lines[:count] * 256.0 + lines[count:2 * count]
    return jnp.concatenate([whole[i:i + 1] for i in range(count)], axis=1)


def pack_kernel(panel, wanted, out, sem):
    rows = panel.shape[0]
    copy = pltpu.make_async_copy(panel, out.at[pl.ds(0, rows)], sem)
    copy.start()
    out[rows:, :] = digits(wanted[...])
    copy.wait()


def place(part, block, depth, first):
    reps = LANES // depth
    row = lax.broadcasted_iota(jnp.int32, (LANES, part.shape[1]), 0)
    inside = (row // depth) == first
    spread = []
    for p in range(2):
        rows = part[(2 * block + p) * depth:(2 * block + p + 1) * depth, :].astype(F32)
        spread.append(jnp.where(inside, jnp.concatenate([rows] * reps, axis=0), 0.0))
    upper = jnp.concatenate([spread[0], spread[1]], axis=1)
    lower = jnp.concatenate([-spread[1], spread[0]], axis=1)
    return jnp.concatenate([upper, lower], axis=0).astype(BF16)


def accumulate(slots, cols, tiles, shards, acc, weights):
    blocks = weights.shape[0]
    starts = []
    for s, (row, depth, parts) in enumerate(shards):
        reps = LANES // depth
        starts.append(pl.multiple_of(row // reps * LANES, LANES))
        share = blocks // len(parts)
        for b in range(blocks):
            weights[b, s * 2 * LANES:(s + 1) * 2 * LANES, :] = place(
                parts[b // share], b % share, depth, row % reps
            )
    for t in range(tiles.shape[0]):
        left = jnp.concatenate(
            [tiles[t, p, :, pl.ds(start, LANES)] for start in starts for p in range(2)], axis=1
        )
        acc[slots[t]] += jnp.dot(left, weights[cols[t]], preferred_element_type=F32)


def hop_first(slots, cols, own, tiles, out, weights, *, n, depth):
    out[...] = jnp.zeros_like(out)
    accumulate(slots, cols, tiles, [(shard_row(n, 0), depth, [own])], out, weights)


def hop_middle(slots, cols, from_left, from_right, tiles, start, out, weights, *, n, depth, hop):
    del start
    shards = [
        (shard_row(n, -hop), depth, [from_left]), (shard_row(n, hop), depth, [from_right])
    ]
    accumulate(slots, cols, tiles, shards, out, weights)


def hop_last(
    slots, cols, pole_weight, low, high, tiles, start, dens, mine, other, acc, weights, *, n, depth
):
    acc[...] = start[...]
    accumulate(slots, cols, tiles, [(shard_row(n, n // 2), depth, [low, high])], acc, weights)
    col = lax.axis_index("col")
    half = mine.shape[2]
    width = mine.shape[3]
    for slot in range(acc.shape[0]):
        real = -acc[slot, :, :width]
        imag = -acc[slot, :, width:]
        dens[slot] = pole_weight[0] * imag + pole_weight[1] * real
        for p in range(2):
            cut = slice(p * width, (p + 1) * width)
            mine[slot, p] = -acc[slot, pl.ds(pl.multiple_of(col * half, half), half), cut]
            other[slot, p] = -acc[slot, pl.ds(pl.multiple_of((1 - col) * half, half), half), cut]


def earlier(total):
    first = lax.broadcasted_iota(jnp.int32, (total, total), 0)
    second = lax.broadcasted_iota(jnp.int32, (total, total), 1)
    return (first < second).astype(F32).astype(BF16)


def basis_kernel(wanted, basis, out, *, n, rows_chip, slots):
    boxes, orbitals, _ = basis.shape
    total = boxes * orbitals
    rows = wanted[...]
    asked = jnp.concatenate([rows[b:b + 1] for b in range(boxes)], axis=1)
    source = asked // rows_chip
    marks = (lax.broadcasted_iota(jnp.int32, (n, total), 0) == source).astype(F32)
    counts = jnp.dot(marks.astype(BF16), earlier(total), preferred_element_type=F32)
    rank = jnp.sum(marks * counts, axis=0, keepdims=True).astype(jnp.int32)
    slot = source * slots + rank
    index = lax.broadcasted_iota(jnp.int32, (out.shape[1], orbitals), 0)
    for b in range(boxes):
        pick = (index == slot[:, b * orbitals:(b + 1) * orbitals]).astype(F32).astype(BF16)
        out[b] = jnp.dot(pick, basis[b], preferred_element_type=F32).astype(BF16)


def pick_kernel(*refs, n, hops, total, rows_chip, slots):
    *shards, out = refs
    lines = -(-2 * total // (16 * LANES)) * 16
    asked = jnp.concatenate(
        [undigits(ref[ref.shape[0] - lines:, :], total) for ref in shards], axis=0
    ).astype(jnp.int32)
    here = (asked // rows_chip) == lax.axis_index("row")
    local = (asked % rows_chip).astype(F32)
    rank = jnp.dot(
        here.astype(F32).astype(BF16), earlier(total), preferred_element_type=F32
    ).astype(jnp.int32)
    rank = jnp.where(here, rank, -1)
    index = lax.broadcasted_iota(jnp.int32, (slots, total), 0)
    lane = lax.broadcasted_iota(jnp.int32, (slots, rows_chip), 1)
    for d, hop in enumerate(hops):
        chosen = jnp.where(index == rank[d:d + 1], local[d:d + 1], 0.0)
        row = jnp.sum(chosen, axis=1, keepdims=True).astype(jnp.int32)
        at = pl.multiple_of(shard_row(n, hop) * slots, slots)
        out[pl.ds(at, slots), :] = (lane == row).astype(F32).astype(BF16)


def select_kernel(pick, mine, theirs, out):
    rows = pick.shape[1]
    total = (mine[...] + theirs[...]).reshape(rows, mine.shape[2]).astype(BF16)
    out[...] = jnp.dot(pick[...], total, preferred_element_type=F32).astype(BF16)


def density_kernel(arrived, basis, supernode, out):
    for n in range(basis.shape[0]):
        projected = lax.dot_general(
            arrived[...], basis[n], (((0,), (0,)), ((), ())), preferred_element_type=F32
        )
        out[n:n + 1, :] = jnp.sum(supernode[n].astype(F32) * projected, axis=0, keepdims=True)


def local(n_row, panel, tiles, tile_slot, tile_col, pole_weight, box_orbitals, box_basis, supernode_basis):
    order = ring_order(n_row)
    half_ring = n_row // 2
    to_right = [(order[i], order[(i + 1) % n_row]) for i in range(n_row)]
    to_left = [(order[(i + 1) % n_row], order[i]) for i in range(n_row)]
    _, blocks, parts, depth, width = panel.shape
    tile_count, _, order_b, _ = tiles.shape
    boxes, orbitals = box_orbitals.shape
    total = boxes * orbitals
    rows_chip = BR_DEV * order_b
    slots = 2 * total // n_row
    arrive = n_row * slots
    half = order_b // 2
    shard_rows = blocks * parts * depth
    lines = -(-2 * total // (16 * LANES)) * 16
    acc_shape = (BR_DEV, order_b, 2 * width)
    acc_out = jax.ShapeDtypeStruct(acc_shape, F32)
    in_vmem = pl.BlockSpec(memory_space=pltpu.VMEM)
    in_smem = pl.BlockSpec(memory_space=pltpu.SMEM)
    in_hbm = pl.BlockSpec(memory_space=pltpu.HBM)
    params = pltpu.CompilerParams(vmem_limit_bytes=VMEM_LIMIT)
    cost = pl.CostEstimate(flops=2 ** 20, bytes_accessed=2 ** 20, transcendentals=0)

    def call(body, in_specs, out_shape, before, shards, aliases={}):
        weights = pltpu.VMEM((blocks, shards * 2 * LANES, 2 * width), BF16)
        return pl.pallas_call(
            functools.partial(body, n=n_row, depth=depth),
            in_specs=in_specs,
            out_specs=jax.tree.map(lambda _: in_vmem, out_shape),
            out_shape=out_shape,
            scratch_shapes=[*before, weights],
            input_output_aliases=aliases,
            compiler_params=params,
            cost_estimate=cost,
        )

    own = pl.pallas_call(
        pack_kernel,
        in_specs=[in_hbm, in_vmem],
        out_specs=in_vmem,
        out_shape=jax.ShapeDtypeStruct((shard_rows + lines, width), BF16),
        scratch_shapes=[pltpu.SemaphoreType.DMA],
        compiler_params=params,
        cost_estimate=cost,
    )(panel.reshape(shard_rows, width), box_orbitals)

    left, right = own, own
    seen, hops = [own], [0]
    acc = None
    for h in range(1, half_ring + 1):
        if h < half_ring:
            next_left = lax.ppermute(left, "row", to_right)
            next_right = lax.ppermute(right, "row", to_left)
        else:
            cut = shard_rows // 2
            next_left = lax.ppermute(left[:cut], "row", to_right)
            next_right = lax.ppermute(right[cut:], "row", to_left)
        if h == 1:
            acc = call(hop_first, [in_smem] * 2 + [in_vmem] * 2, acc_out, [], 1)(
                tile_slot, tile_col, own, tiles
            )
        else:
            acc = call(
                functools.partial(hop_middle, hop=h - 1),
                [in_smem] * 2 + [in_vmem] * 4,
                acc_out,
                [],
                2,
                aliases={5: 0},
            )(tile_slot, tile_col, left, right, tiles, acc)
        left, right, acc = lax.optimization_barrier((next_left, next_right, acc))
        if h < half_ring:
            seen += [left, right]
            hops += [-h, h]
        else:
            seen.append(right)
            hops.append(h)

    half_shape = (BR_DEV, 2, half, width)
    dens_shape = (BR_DEV, order_b, width)
    dens, mine, other = call(
        hop_last,
        [in_smem] * 3 + [in_vmem] * 4,
        [
            jax.ShapeDtypeStruct(dens_shape, F32),
            jax.ShapeDtypeStruct(half_shape, F32),
            jax.ShapeDtypeStruct(half_shape, F32),
        ],
        [pltpu.VMEM(acc_shape, F32)],
        1,
    )(tile_slot, tile_col, pole_weight, left, right, tiles, acc)

    basis_here = pl.pallas_call(
        functools.partial(basis_kernel, n=n_row, rows_chip=rows_chip, slots=slots),
        out_shape=jax.ShapeDtypeStruct((boxes, arrive, box_basis.shape[2]), BF16),
        compiler_params=params,
        cost_estimate=cost,
    )(box_orbitals, box_basis)
    pick = pl.pallas_call(
        functools.partial(
            pick_kernel, n=n_row, hops=hops, total=total, rows_chip=rows_chip, slots=slots
        ),
        out_shape=jax.ShapeDtypeStruct((arrive, rows_chip), BF16),
        compiler_params=params,
        cost_estimate=cost,
    )(*seen)

    swap = [(0, 1), (1, 0)]
    dens_other = lax.ppermute(dens, "col", swap)
    inverse_other = lax.ppermute(other, "col", swap)
    send = pl.pallas_call(
        select_kernel,
        out_shape=jax.ShapeDtypeStruct((arrive, width), BF16),
        compiler_params=params,
    )(pick, dens, dens_other)
    arrived = lax.all_to_all(send, "row", 0, 0, tiled=True)
    density = pl.pallas_call(
        density_kernel,
        out_shape=jax.ShapeDtypeStruct((boxes, box_basis.shape[2]), F32),
        compiler_params=params,
    )(arrived, basis_here, supernode_basis)
    return mine + inverse_other, density


def solution(mesh):
    return jax.shard_map(
        functools.partial(local, mesh.shape["row"]),
        mesh=mesh,
        in_specs=(
            P(("pole", "col"), None, None, "row", None),
            P(("pole", "row", "col"), None, None, None),
            P(("pole", "row", "col")),
            P(("pole", "row", "col")),
            P("pole"),
            P(("pole", "row", "col"), None),
            P(("pole", "row", "col"), None, None),
            P(("pole", "row", "col"), None, None),
        ),
        out_specs=(P(("pole", "row"), None, "col", None), P(("pole", "row", "col"), None)),
        check_vma=False,
    )
```

```python
import functools

import jax
import jax.numpy as jnp
from jax import lax
from jax.experimental import pallas as pl
from jax.experimental.pallas import tpu as pltpu
from jax.sharding import PartitionSpec as P

BR_DEV = 2
LANES = 128
F32 = jnp.float32
BF16 = jnp.bfloat16
VMEM_LIMIT = 8 * 1024 * 1024
PACK_LIMIT = 56 * 1024 * 1024


def ring_order(n):
    if n <= 8 and n % 2 == 0:
        return list(range(0, n, 2)) + list(range(n - 1, 0, -2))
    return list(range(n))


def shard_row(n, hop):
    row = lax.axis_index("row")
    if ring_order(n) == list(range(n)):
        return lax.rem(row + hop + n, n)
    at = jnp.where(row % 2 == 0, row // 2, n - 1 - row // 2)
    at = lax.rem(at + hop + n, n)
    return jnp.where(at < n // 2, 2 * at, 2 * (n - 1 - at) + 1)


def digits(rows):
    boxes, orbitals = rows.shape
    pieces = [rows[n:n + 1, c:c + LANES] for n in range(boxes) for c in range(0, orbitals, LANES)]
    lines = [piece // 256 for piece in pieces] + [piece % 256 for piece in pieces]
    pad = -len(lines) % 16
    lines.append(jnp.zeros((pad, LANES), jnp.int32))
    return jnp.concatenate(lines, axis=0).astype(F32).astype(BF16)


def undigits(lines, total):
    count = total // LANES
    lines = lines.astype(F32)
    whole = lines[:count] * 256.0 + lines[count:2 * count]
    return jnp.concatenate([whole[i:i + 1] for i in range(count)], axis=1)


def pack_kernel(panel, wanted, out, held, sems):
    rows = panel.shape[0]
    bring = pltpu.make_async_copy(wanted, held, sems.at[0])
    copy = pltpu.make_async_copy(panel, out.at[pl.ds(0, rows)], sems.at[1])
    bring.start()
    copy.start()
    bring.wait()
    out[rows:, :] = digits(held[...])
    copy.wait()


def place(part, block, depth, first):
    reps = LANES // depth
    row = lax.broadcasted_iota(jnp.int32, (LANES, part.shape[1]), 0)
    inside = (row // depth) == first
    spread = []
    for p in range(2):
        rows = part[(2 * block + p) * depth:(2 * block + p + 1) * depth, :].astype(F32)
        spread.append(jnp.where(inside, jnp.concatenate([rows] * reps, axis=0), 0.0))
    upper = jnp.concatenate([spread[0], spread[1]], axis=1)
    lower = jnp.concatenate([-spread[1], spread[0]], axis=1)
    return jnp.concatenate([upper, lower], axis=0).astype(BF16)


def accumulate(slots, cols, tiles, shards, acc, weights):
    blocks = weights.shape[0]
    starts = []
    for s, (row, depth, parts) in enumerate(shards):
        reps = LANES // depth
        starts.append(pl.multiple_of(row // reps * LANES, LANES))
        share = blocks // len(parts)
        for b in range(blocks):
            weights[b, s * 2 * LANES:(s + 1) * 2 * LANES, :] = place(
                parts[b // share], b % share, depth, row % reps
            )
    for t in range(tiles.shape[0]):
        left = jnp.concatenate(
            [tiles[t, p, :, pl.ds(start, LANES)] for start in starts for p in range(2)], axis=1
        )
        acc[slots[t]] += jnp.dot(left, weights[cols[t]], preferred_element_type=F32)


def stage_kernel(slots, cols, own, tiles, slots_out, cols_out, own_out, out):
    del tiles
    slots_out[...] = slots[...]
    cols_out[...] = cols[...]
    own_out[...] = own[...]
    out[...] = jnp.zeros_like(out)


def hop_early(slots, cols, own, from_left, from_right, tiles, start, out, weights, *, n, depth):
    del start
    shards = [
        (shard_row(n, 0), depth, [own]),
        (shard_row(n, -1), depth, [from_left]),
        (shard_row(n, 1), depth, [from_right]),
    ]
    accumulate(slots, cols, tiles, shards, out, weights)


def hop_middle(slots, cols, from_left, from_right, tiles, start, out, weights, *, n, depth, hop):
    del start
    shards = [
        (shard_row(n, -hop), depth, [from_left]), (shard_row(n, hop), depth, [from_right])
    ]
    accumulate(slots, cols, tiles, shards, out, weights)


def hop_last(slots, cols, pole_weight, low, high, tiles, start, out, dens, weights, *, n, depth):
    del start
    accumulate(slots, cols, tiles, [(shard_row(n, n // 2), depth, [low, high])], out, weights)
    width = dens.shape[2]
    for slot in range(out.shape[0]):
        dens[slot] = -(pole_weight[0] * out[slot, :, width:] + pole_weight[1] * out[slot, :, :width])


def halves_kernel(acc, mine, other):
    col = lax.axis_index("col")
    half = mine.shape[2]
    width = mine.shape[3]
    for slot in range(acc.shape[0]):
        for p in range(2):
            cut = slice(p * width, (p + 1) * width)
            mine[slot, p] = -acc[slot, pl.ds(pl.multiple_of(col * half, half), half), cut]
            other[slot, p] = -acc[slot, pl.ds(pl.multiple_of((1 - col) * half, half), half), cut]


def earlier(total):
    first = lax.broadcasted_iota(jnp.int32, (total, total), 0)
    second = lax.broadcasted_iota(jnp.int32, (total, total), 1)
    return (first < second).astype(F32).astype(BF16)


def basis_kernel(wanted, basis, supernode, out, wide, *, n, rows_chip, slots):
    wide[...] = supernode[...].astype(F32)
    boxes, orbitals, _ = basis.shape
    total = boxes * orbitals
    rows = wanted[...]
    asked = jnp.concatenate([rows[b:b + 1] for b in range(boxes)], axis=1)
    source = asked // rows_chip
    marks = (lax.broadcasted_iota(jnp.int32, (n, total), 0) == source).astype(F32)
    counts = jnp.dot(marks.astype(BF16), earlier(total), preferred_element_type=F32)
    rank = jnp.sum(marks * counts, axis=0, keepdims=True).astype(jnp.int32)
    slot = source * slots + rank
    index = lax.broadcasted_iota(jnp.int32, (out.shape[1], orbitals), 0)
    for b in range(boxes):
        pick = (index == slot[:, b * orbitals:(b + 1) * orbitals]).astype(F32).astype(BF16)
        out[b] = jnp.dot(pick, basis[b], preferred_element_type=F32).astype(BF16)


def pick_kernel(*refs, n, hops, total, rows_chip, slots):
    *shards, out = refs
    lines = -(-2 * total // (16 * LANES)) * 16
    asked = jnp.concatenate(
        [undigits(ref[ref.shape[0] - lines:, :], total) for ref in shards], axis=0
    ).astype(jnp.int32)
    here = (asked // rows_chip) == lax.axis_index("row")
    local = (asked % rows_chip).astype(F32)
    rank = jnp.dot(
        here.astype(F32).astype(BF16), earlier(total), preferred_element_type=F32
    ).astype(jnp.int32)
    rank = jnp.where(here, rank, -1)
    index = lax.broadcasted_iota(jnp.int32, (slots, total), 0)
    lane = lax.broadcasted_iota(jnp.int32, (slots, rows_chip), 1)
    for d, hop in enumerate(hops):
        chosen = jnp.where(index == rank[d:d + 1], local[d:d + 1], 0.0)
        row = jnp.sum(chosen, axis=1, keepdims=True).astype(jnp.int32)
        at = pl.multiple_of(shard_row(n, hop) * slots, slots)
        out[pl.ds(at, slots), :] = (lane == row).astype(F32).astype(BF16)


def add_kernel(mine, theirs, out):
    out[...] = mine[...] + theirs[...]


def select_kernel(pick, mine, theirs, out):
    rows = pick.shape[1]
    total = (mine[...] + theirs[...]).reshape(rows, mine.shape[2]).astype(BF16)
    out[...] = jnp.dot(pick[...], total, preferred_element_type=F32).astype(BF16)


def density_kernel(arrived, basis, supernode, out):
    for n in range(basis.shape[0]):
        projected = lax.dot_general(
            arrived[...], basis[n], (((0,), (0,)), ((), ())), preferred_element_type=F32
        )
        out[n:n + 1, :] = jnp.sum(supernode[n] * projected, axis=0, keepdims=True)


def local(n_row, panel, tiles, tile_slot, tile_col, pole_weight, box_orbitals, box_basis, supernode_basis):
    order = ring_order(n_row)
    half_ring = n_row // 2
    to_right = [(order[i], order[(i + 1) % n_row]) for i in range(n_row)]
    to_left = [(order[(i + 1) % n_row], order[i]) for i in range(n_row)]
    _, blocks, parts, depth, width = panel.shape
    tile_count, _, order_b, _ = tiles.shape
    boxes, orbitals = box_orbitals.shape
    total = boxes * orbitals
    rows_chip = BR_DEV * order_b
    slots = 2 * total // n_row
    arrive = n_row * slots
    half = order_b // 2
    shard_rows = blocks * parts * depth
    lines = -(-2 * total // (16 * LANES)) * 16
    acc_shape = (BR_DEV, order_b, 2 * width)
    acc_out = jax.ShapeDtypeStruct(acc_shape, F32)
    in_vmem = pl.BlockSpec(memory_space=pltpu.VMEM)
    in_smem = pl.BlockSpec(memory_space=pltpu.SMEM)
    in_hbm = pl.BlockSpec(memory_space=pltpu.HBM)
    params = pltpu.CompilerParams(vmem_limit_bytes=VMEM_LIMIT)
    cost = pl.CostEstimate(flops=2 ** 20, bytes_accessed=2 ** 20, transcendentals=0)

    def call(body, in_specs, out_shape, before, shards, aliases={}):
        weights = pltpu.VMEM((blocks, shards * 2 * LANES, 2 * width), BF16)
        return pl.pallas_call(
            functools.partial(body, n=n_row, depth=depth),
            in_specs=in_specs,
            out_specs=jax.tree.map(lambda _: in_vmem, out_shape),
            out_shape=out_shape,
            scratch_shapes=[*before, weights],
            input_output_aliases=aliases,
            compiler_params=params,
            cost_estimate=cost,
        )

    own = pl.pallas_call(
        pack_kernel,
        in_specs=[in_hbm, in_hbm],
        out_specs=in_vmem,
        out_shape=jax.ShapeDtypeStruct((shard_rows + lines, width), BF16),
        scratch_shapes=[pltpu.VMEM(box_orbitals.shape, jnp.int32), pltpu.SemaphoreType.DMA((2,))],
        compiler_params=pltpu.CompilerParams(vmem_limit_bytes=PACK_LIMIT),
        cost_estimate=cost,
    )(panel.reshape(shard_rows, width), box_orbitals)

    left, right = own, own
    seen, hops = [own], [0]
    acc = None
    for h in range(1, half_ring + 1):
        if h < half_ring:
            next_left = lax.ppermute(left, "row", to_right)
            next_right = lax.ppermute(right, "row", to_left)
        else:
            cut = shard_rows // 2
            next_left = lax.ppermute(left[:cut], "row", to_right)
            next_right = lax.ppermute(right[cut:], "row", to_left)
        if h == 1:
            tile_slot, tile_col, own, acc = pl.pallas_call(
                stage_kernel,
                in_specs=[in_vmem] * 4,
                out_specs=[in_vmem] * 4,
                out_shape=[
                    jax.ShapeDtypeStruct(tile_slot.shape, jnp.int32),
                    jax.ShapeDtypeStruct(tile_col.shape, jnp.int32),
                    jax.ShapeDtypeStruct(own.shape, BF16),
                    acc_out,
                ],
                compiler_params=params,
                cost_estimate=cost,
            )(tile_slot, tile_col, own, tiles)
            seen[0] = own
        elif h == 2:
            acc = call(
                hop_early, [in_smem] * 2 + [in_vmem] * 5, acc_out, [], 3, aliases={6: 0}
            )(tile_slot, tile_col, own, left, right, tiles, acc)
        elif h > 2:
            acc = call(
                functools.partial(hop_middle, hop=h - 1),
                [in_smem] * 2 + [in_vmem] * 4,
                acc_out,
                [],
                2,
                aliases={5: 0},
            )(tile_slot, tile_col, left, right, tiles, acc)
        left, done = lax.optimization_barrier((next_left, acc))
        right, _ = lax.optimization_barrier((next_right, acc))
        acc = done
        if h < half_ring:
            seen += [left, right]
            hops += [-h, h]
        else:
            seen.append(right)
            hops.append(h)

    half_shape = (BR_DEV, 2, half, width)
    acc, dens = call(
        hop_last,
        [in_smem] * 3 + [in_vmem] * 4,
        [acc_out, jax.ShapeDtypeStruct((BR_DEV, order_b, width), F32)],
        [],
        1,
        aliases={6: 0},
    )(tile_slot, tile_col, pole_weight, left, right, tiles, acc)
    mine, other = pl.pallas_call(
        halves_kernel,
        out_shape=[jax.ShapeDtypeStruct(half_shape, F32)] * 2,
        compiler_params=params,
        cost_estimate=cost,
    )(acc)

    basis_here, wide = pl.pallas_call(
        functools.partial(basis_kernel, n=n_row, rows_chip=rows_chip, slots=slots),
        out_shape=[
            jax.ShapeDtypeStruct((boxes, arrive, box_basis.shape[2]), BF16),
            jax.ShapeDtypeStruct(supernode_basis.shape, F32),
        ],
        compiler_params=params,
        cost_estimate=cost,
    )(box_orbitals, box_basis, supernode_basis)
    pick = pl.pallas_call(
        functools.partial(
            pick_kernel, n=n_row, hops=hops, total=total, rows_chip=rows_chip, slots=slots
        ),
        out_shape=jax.ShapeDtypeStruct((arrive, rows_chip), BF16),
        compiler_params=params,
        cost_estimate=cost,
    )(*seen)

    swap = [(0, 1), (1, 0)]
    dens_other = lax.ppermute(dens, "col", swap)
    inverse_other = lax.ppermute(other, "col", swap)
    send = pl.pallas_call(
        select_kernel,
        out_shape=jax.ShapeDtypeStruct((arrive, width), BF16),
        compiler_params=params,
    )(pick, dens, dens_other)
    arrived = lax.all_to_all(send, "row", 0, 0, tiled=True)
    inverse = pl.pallas_call(
        add_kernel,
        out_shape=jax.ShapeDtypeStruct(half_shape, F32),
        compiler_params=params,
        cost_estimate=cost,
    )(mine, inverse_other)
    density = pl.pallas_call(
        density_kernel,
        out_shape=jax.ShapeDtypeStruct((boxes, box_basis.shape[2]), F32),
        compiler_params=params,
    )(arrived, basis_here, wide)
    return inverse, density


def solution(mesh):
    return jax.shard_map(
        functools.partial(local, mesh.shape["row"]),
        mesh=mesh,
        in_specs=(
            P(("pole", "col"), None, None, "row", None),
            P(("pole", "row", "col"), None, None, None),
            P(("pole", "row", "col")),
            P(("pole", "row", "col")),
            P("pole"),
            P(("pole", "row", "col"), None),
            P(("pole", "row", "col"), None, None),
            P(("pole", "row", "col"), None, None),
        ),
        out_specs=(P(("pole", "row"), None, "col", None), P(("pole", "row", "col"), None)),
        check_vma=False,
    )
```

```python
import functools

import jax
import jax.numpy as jnp
from jax import lax
from jax.experimental import pallas as pl
from jax.experimental.pallas import tpu as pltpu
from jax.sharding import PartitionSpec as P

BR_DEV = 2
LANES = 128
F32 = jnp.float32
BF16 = jnp.bfloat16
VMEM_LIMIT = 8 * 1024 * 1024
PACK_LIMIT = 8 * 1024 * 1024


def ring_order(n):
    if n <= 8 and n % 2 == 0:
        return list(range(0, n, 2)) + list(range(n - 1, 0, -2))
    return list(range(n))


def shard_row(n, hop):
    row = lax.axis_index("row")
    if ring_order(n) == list(range(n)):
        return lax.rem(row + hop + n, n)
    at = jnp.where(row % 2 == 0, row // 2, n - 1 - row // 2)
    at = lax.rem(at + hop + n, n)
    return jnp.where(at < n // 2, 2 * at, 2 * (n - 1 - at) + 1)


def digits(rows):
    boxes, orbitals = rows.shape
    pieces = [rows[n:n + 1, c:c + LANES] for n in range(boxes) for c in range(0, orbitals, LANES)]
    lines = [piece // 256 for piece in pieces] + [piece % 256 for piece in pieces]
    pad = -len(lines) % 16
    lines.append(jnp.zeros((pad, LANES), jnp.int32))
    return jnp.concatenate(lines, axis=0).astype(F32).astype(BF16)


def undigits(lines, total):
    count = total // LANES
    lines = lines.astype(F32)
    whole = lines[:count] * 256.0 + lines[count:2 * count]
    return jnp.concatenate([whole[i:i + 1] for i in range(count)], axis=1)


def pack_kernel(panel, wanted, out, held, sems):
    rows = panel.shape[0]
    bring = pltpu.make_async_copy(wanted, held, sems.at[0])
    copy = pltpu.make_async_copy(panel, out.at[pl.ds(0, rows)], sems.at[1])
    bring.start()
    copy.start()
    bring.wait()
    out[rows:, :] = digits(held[...])
    copy.wait()


def place(part, block, depth, first):
    reps = LANES // depth
    row = lax.broadcasted_iota(jnp.int32, (LANES, part.shape[1]), 0)
    inside = (row // depth) == first
    spread = []
    for p in range(2):
        rows = part[(2 * block + p) * depth:(2 * block + p + 1) * depth, :].astype(F32)
        spread.append(jnp.where(inside, jnp.concatenate([rows] * reps, axis=0), 0.0))
    upper = jnp.concatenate([spread[0], spread[1]], axis=1)
    lower = jnp.concatenate([-spread[1], spread[0]], axis=1)
    return jnp.concatenate([upper, lower], axis=0).astype(BF16)


def accumulate(slots, cols, tiles, shards, acc, weights):
    blocks = weights.shape[0]
    starts = []
    for s, (row, depth, parts) in enumerate(shards):
        reps = LANES // depth
        starts.append(pl.multiple_of(row // reps * LANES, LANES))
        share = blocks // len(parts)
        for b in range(blocks):
            weights[b, s * 2 * LANES:(s + 1) * 2 * LANES, :] = place(
                parts[b // share], b % share, depth, row % reps
            )
    for t in range(tiles.shape[0]):
        left = jnp.concatenate(
            [tiles[t, p, :, pl.ds(start, LANES)] for start in starts for p in range(2)], axis=1
        )
        acc[slots[t]] += jnp.dot(left, weights[cols[t]], preferred_element_type=F32)


def stage_kernel(slots, cols, own, tiles, slots_out, cols_out, own_out, out):
    del tiles
    slots_out[...] = slots[...]
    cols_out[...] = cols[...]
    own_out[...] = own[...]
    out[...] = jnp.zeros_like(out)


def hop_early(slots, cols, own, from_left, from_right, tiles, start, out, weights, *, n, depth):
    del start
    shards = [
        (shard_row(n, 0), depth, [own]),
        (shard_row(n, -1), depth, [from_left]),
        (shard_row(n, 1), depth, [from_right]),
    ]
    accumulate(slots, cols, tiles, shards, out, weights)


def hop_middle(slots, cols, from_left, from_right, tiles, start, out, weights, *, n, depth, hop):
    del start
    shards = [
        (shard_row(n, -hop), depth, [from_left]), (shard_row(n, hop), depth, [from_right])
    ]
    accumulate(slots, cols, tiles, shards, out, weights)


def hop_last(slots, cols, pole_weight, low, high, tiles, start, out, dens, weights, *, n, depth):
    del start
    accumulate(slots, cols, tiles, [(shard_row(n, n // 2), depth, [low, high])], out, weights)
    width = dens.shape[2]
    for slot in range(out.shape[0]):
        dens[slot] = -(pole_weight[0] * out[slot, :, width:] + pole_weight[1] * out[slot, :, :width])


def halves_kernel(acc, mine, other):
    col = lax.axis_index("col")
    half = mine.shape[2]
    width = mine.shape[3]
    for slot in range(acc.shape[0]):
        for p in range(2):
            cut = slice(p * width, (p + 1) * width)
            mine[slot, p] = -acc[slot, pl.ds(pl.multiple_of(col * half, half), half), cut]
            other[slot, p] = -acc[slot, pl.ds(pl.multiple_of((1 - col) * half, half), half), cut]


def earlier(total):
    first = lax.broadcasted_iota(jnp.int32, (total, total), 0)
    second = lax.broadcasted_iota(jnp.int32, (total, total), 1)
    return (first < second).astype(F32).astype(BF16)


def place_of(chip, n):
    apart = chip ^ lax.axis_index("row")
    top = (apart >= n // 2).astype(jnp.int32)
    step = jnp.where(top == 1, apart - n // 2, apart - 1)
    other = (top != lax.axis_index("col")).astype(jnp.int32)
    return jnp.where(apart == 0, 0, 1 + other * (n // 2) + step)


def basis_kernel(wanted, basis, supernode, out, wide, *, n, rows_chip, slots):
    wide[...] = supernode[...].astype(F32)
    boxes, orbitals, _ = basis.shape
    total = boxes * orbitals
    rows = wanted[...]
    asked = jnp.concatenate([rows[b:b + 1] for b in range(boxes)], axis=1)
    source = asked // rows_chip
    marks = (lax.broadcasted_iota(jnp.int32, (n, total), 0) == source).astype(F32)
    counts = jnp.dot(marks.astype(BF16), earlier(total), preferred_element_type=F32)
    rank = jnp.sum(marks * counts, axis=0, keepdims=True).astype(jnp.int32)
    slot = place_of(source, n) * slots + rank
    index = lax.broadcasted_iota(jnp.int32, (out.shape[1], orbitals), 0)
    for b in range(boxes):
        pick = (index == slot[:, b * orbitals:(b + 1) * orbitals]).astype(F32).astype(BF16)
        out[b] = jnp.dot(pick, basis[b], preferred_element_type=F32).astype(BF16)


def lines_kernel(*refs, n, hops, lines):
    *shards, out = refs
    for ref, hop in zip(shards, hops):
        at = pl.multiple_of(shard_row(n, hop) * lines, lines)
        out[pl.ds(at, lines), :] = ref[ref.shape[0] - lines:, :]


def pick_kernel(mine, theirs, out, *, n, lines, total, rows_chip, slots):
    row = lax.axis_index("row")
    col = lax.axis_index("col")
    first = jnp.where(col == 0, 1, n // 2)

    def asked_by(chip, own):
        at = pl.ds(pl.multiple_of(chip * lines, lines), lines)
        return undigits(jnp.where(own, mine[at, :].astype(F32), theirs[at, :].astype(F32)), total)

    asked = [asked_by(row, True)]
    for step in range(n // 2):
        chip = row ^ jnp.minimum(first + step, n - 1)
        asked += [asked_by(chip, col == 0), asked_by(chip, col == 1)]
    count = len(asked)
    asked = jnp.concatenate(asked, axis=0).astype(jnp.int32)
    here = (asked // rows_chip) == row
    local = (asked % rows_chip).astype(F32)
    rank = jnp.dot(
        here.astype(F32).astype(BF16), earlier(total), preferred_element_type=F32
    ).astype(jnp.int32)
    rank = jnp.where(here, rank, -1)
    index = lax.broadcasted_iota(jnp.int32, (slots, total), 0)
    lane = lax.broadcasted_iota(jnp.int32, (slots, rows_chip), 1)
    for d in range(count):
        chosen = jnp.where(index == rank[d:d + 1], local[d:d + 1], 0.0)
        at = jnp.sum(chosen, axis=1, keepdims=True).astype(jnp.int32)
        out[d * slots:(d + 1) * slots, :] = (lane == at).astype(F32).astype(BF16)


def add_kernel(mine, theirs, out):
    out[...] = mine[...] + theirs[...]


def select_kernel(pick, mine, theirs, *outs):
    rows = pick.shape[1]
    total = (mine[...] + theirs[...]).reshape(rows, mine.shape[2]).astype(BF16)
    rows_out = jnp.dot(pick[...], total, preferred_element_type=F32).astype(BF16)
    at = 0
    for out in outs:
        out[...] = rows_out[at:at + out.shape[0]]
        at += out.shape[0]


def density_kernel(*refs):
    *parts, basis, supernode, out = refs
    own = parts[0]
    slots = own.shape[0]
    at = pl.ds(pl.multiple_of(lax.axis_index("col") * slots, slots), slots)
    arrived = jnp.concatenate([own[...]] + [part[at, :] for part in parts[1:]], axis=0)
    for n in range(basis.shape[0]):
        projected = lax.dot_general(
            arrived, basis[n], (((0,), (0,)), ((), ())), preferred_element_type=F32
        )
        out[n:n + 1, :] = jnp.sum(supernode[n] * projected, axis=0, keepdims=True)


def local(n_row, panel, tiles, tile_slot, tile_col, pole_weight, box_orbitals, box_basis, supernode_basis):
    order = ring_order(n_row)
    half_ring = n_row // 2
    to_right = [(order[i], order[(i + 1) % n_row]) for i in range(n_row)]
    to_left = [(order[(i + 1) % n_row], order[i]) for i in range(n_row)]
    _, blocks, parts, depth, width = panel.shape
    tile_count, _, order_b, _ = tiles.shape
    boxes, orbitals = box_orbitals.shape
    total = boxes * orbitals
    rows_chip = BR_DEV * order_b
    slots = 2 * total // n_row
    arrive = (1 + 2 * half_ring) * slots
    half = order_b // 2
    shard_rows = blocks * parts * depth
    lines = -(-2 * total // (16 * LANES)) * 16
    acc_shape = (BR_DEV, order_b, 2 * width)
    acc_out = jax.ShapeDtypeStruct(acc_shape, F32)
    in_vmem = pl.BlockSpec(memory_space=pltpu.VMEM)
    in_smem = pl.BlockSpec(memory_space=pltpu.SMEM)
    in_hbm = pl.BlockSpec(memory_space=pltpu.HBM)
    params = pltpu.CompilerParams(vmem_limit_bytes=VMEM_LIMIT)
    cost = pl.CostEstimate(flops=2 ** 20, bytes_accessed=2 ** 20, transcendentals=0)

    def call(body, in_specs, out_shape, before, shards, aliases={}):
        weights = pltpu.VMEM((blocks, shards * 2 * LANES, 2 * width), BF16)
        return pl.pallas_call(
            functools.partial(body, n=n_row, depth=depth),
            in_specs=in_specs,
            out_specs=jax.tree.map(lambda _: in_vmem, out_shape),
            out_shape=out_shape,
            scratch_shapes=[*before, weights],
            input_output_aliases=aliases,
            compiler_params=params,
            cost_estimate=cost,
        )

    own = pl.pallas_call(
        pack_kernel,
        in_specs=[in_hbm, in_hbm],
        out_specs=in_vmem,
        out_shape=jax.ShapeDtypeStruct((shard_rows + lines, width), BF16),
        scratch_shapes=[pltpu.VMEM(box_orbitals.shape, jnp.int32), pltpu.SemaphoreType.DMA((2,))],
        compiler_params=pltpu.CompilerParams(vmem_limit_bytes=PACK_LIMIT),
        cost_estimate=cost,
    )(panel.reshape(shard_rows, width), box_orbitals)

    basis_here, wide = pl.pallas_call(
        functools.partial(basis_kernel, n=n_row, rows_chip=rows_chip, slots=slots),
        out_shape=[
            jax.ShapeDtypeStruct((boxes, arrive, box_basis.shape[2]), BF16),
            jax.ShapeDtypeStruct(supernode_basis.shape, F32),
        ],
        compiler_params=params,
        cost_estimate=cost,
    )(box_orbitals, box_basis, supernode_basis)

    left, right = own, own
    seen, hops = [own], [0]
    acc = None
    for h in range(1, half_ring + 1):
        if h < half_ring:
            next_left = lax.ppermute(left, "row", to_right)
            next_right = lax.ppermute(right, "row", to_left)
        else:
            cut = shard_rows // 2
            next_left = lax.ppermute(left[:cut], "row", to_right)
            next_right = lax.ppermute(right[cut:], "row", to_left)
        if h == 1:
            tile_slot, tile_col, own, acc = pl.pallas_call(
                stage_kernel,
                in_specs=[in_vmem] * 4,
                out_specs=[in_vmem] * 4,
                out_shape=[
                    jax.ShapeDtypeStruct(tile_slot.shape, jnp.int32),
                    jax.ShapeDtypeStruct(tile_col.shape, jnp.int32),
                    jax.ShapeDtypeStruct(own.shape, BF16),
                    acc_out,
                ],
                compiler_params=params,
                cost_estimate=cost,
            )(tile_slot, tile_col, own, tiles)
            seen[0] = own
        elif h == 2:
            acc = call(
                hop_early, [in_smem] * 2 + [in_vmem] * 5, acc_out, [], 3, aliases={6: 0}
            )(tile_slot, tile_col, own, left, right, tiles, acc)
        elif h > 2:
            acc = call(
                functools.partial(hop_middle, hop=h - 1),
                [in_smem] * 2 + [in_vmem] * 4,
                acc_out,
                [],
                2,
                aliases={5: 0},
            )(tile_slot, tile_col, left, right, tiles, acc)
        if h == half_ring - 1:
            next_left, basis_here, wide = lax.optimization_barrier((next_left, basis_here, wide))
        left, done = lax.optimization_barrier((next_left, acc))
        right, _ = lax.optimization_barrier((next_right, acc))
        acc = done
        if h < half_ring:
            seen += [left, right]
            hops += [-h, h]
        else:
            seen.append(right)
            hops.append(h)

    swap = [(0, 1), (1, 0)]
    wanted = pl.pallas_call(
        functools.partial(lines_kernel, n=n_row, hops=hops, lines=lines),
        out_shape=jax.ShapeDtypeStruct((n_row * lines, width), BF16),
        compiler_params=params,
        cost_estimate=cost,
    )(*seen)
    left, wanted = lax.optimization_barrier((left, wanted))
    wanted_other = lax.ppermute(wanted, "col", swap)

    half_shape = (BR_DEV, 2, half, width)
    acc, dens = call(
        hop_last,
        [in_smem] * 3 + [in_vmem] * 4,
        [acc_out, jax.ShapeDtypeStruct((BR_DEV, order_b, width), F32)],
        [],
        1,
        aliases={6: 0},
    )(tile_slot, tile_col, pole_weight, left, right, tiles, acc)
    dens_other = lax.ppermute(dens, "col", swap)
    pick = pl.pallas_call(
        functools.partial(
            pick_kernel, n=n_row, lines=lines, total=total, rows_chip=rows_chip, slots=slots
        ),
        out_shape=jax.ShapeDtypeStruct((arrive, rows_chip), BF16),
        compiler_params=params,
        cost_estimate=cost,
    )(wanted, wanted_other)
    message = jax.ShapeDtypeStruct((2 * slots, width), BF16)
    kept, *sent = pl.pallas_call(
        select_kernel,
        out_shape=[jax.ShapeDtypeStruct((slots, width), BF16)] + [message] * half_ring,
        compiler_params=params,
        cost_estimate=cost,
    )(pick, dens, dens_other)

    fetched, passed = [], []
    for step in range(half_ring):
        pairs = [(2 * r + 1, 2 * (r ^ (half_ring + step)) + 1) for r in range(n_row)]
        if step + 1 < half_ring:
            pairs += [(2 * r, 2 * (r ^ (1 + step))) for r in range(n_row)]
        fetched.append(lax.ppermute(sent[step], ("row", "col"), pairs))
        passed.append(lax.ppermute(fetched[-1], "col", swap))

    acc, fetched[0] = lax.optimization_barrier((acc, fetched[0]))
    mine, other = pl.pallas_call(
        halves_kernel,
        out_shape=[jax.ShapeDtypeStruct(half_shape, F32)] * 2,
        compiler_params=params,
        cost_estimate=cost,
    )(acc)
    inverse_other = lax.ppermute(other, "col", swap)
    inverse = pl.pallas_call(
        add_kernel,
        out_shape=jax.ShapeDtypeStruct(half_shape, F32),
        compiler_params=params,
        cost_estimate=cost,
    )(mine, inverse_other)
    kept, inverse = lax.optimization_barrier((kept, inverse))
    density = pl.pallas_call(
        density_kernel,
        out_shape=jax.ShapeDtypeStruct((boxes, box_basis.shape[2]), F32),
        compiler_params=params,
    )(kept, *fetched, *passed, basis_here, wide)
    return inverse, density


def solution(mesh):
    return jax.shard_map(
        functools.partial(local, mesh.shape["row"]),
        mesh=mesh,
        in_specs=(
            P(("pole", "col"), None, None, "row", None),
            P(("pole", "row", "col"), None, None, None),
            P(("pole", "row", "col")),
            P(("pole", "row", "col")),
            P("pole"),
            P(("pole", "row", "col"), None),
            P(("pole", "row", "col"), None, None),
            P(("pole", "row", "col"), None, None),
        ),
        out_specs=(P(("pole", "row"), None, "col", None), P(("pole", "row", "col"), None)),
        check_vma=False,
    )
```

```python
import functools

import jax
import jax.numpy as jnp
from jax import lax
from jax.experimental import pallas as pl
from jax.experimental.pallas import tpu as pltpu
from jax.sharding import PartitionSpec as P

BR_DEV = 2
LANES = 128
F32 = jnp.float32
BF16 = jnp.bfloat16
VMEM_LIMIT = 8 * 1024 * 1024
PACK_LIMIT = 8 * 1024 * 1024


def ring_order(n):
    if n <= 8 and n % 2 == 0:
        return list(range(0, n, 2)) + list(range(n - 1, 0, -2))
    return list(range(n))


def shard_row(n, hop):
    row = lax.axis_index("row")
    if ring_order(n) == list(range(n)):
        return lax.rem(row + hop + n, n)
    at = jnp.where(row % 2 == 0, row // 2, n - 1 - row // 2)
    at = lax.rem(at + hop + n, n)
    return jnp.where(at < n // 2, 2 * at, 2 * (n - 1 - at) + 1)


def digits(rows):
    boxes, orbitals = rows.shape
    pieces = [rows[n:n + 1, c:c + LANES] for n in range(boxes) for c in range(0, orbitals, LANES)]
    lines = [piece // 256 for piece in pieces] + [piece % 256 for piece in pieces]
    pad = -len(lines) % 16
    lines.append(jnp.zeros((pad, LANES), jnp.int32))
    return jnp.concatenate(lines, axis=0).astype(F32).astype(BF16)


def undigits(lines, total):
    count = total // LANES
    lines = lines.astype(F32)
    whole = lines[:count] * 256.0 + lines[count:2 * count]
    return jnp.concatenate([whole[i:i + 1] for i in range(count)], axis=1)


def pack_kernel(panel, wanted, out, held, sems):
    rows = panel.shape[0]
    bring = pltpu.make_async_copy(wanted, held, sems.at[0])
    copy = pltpu.make_async_copy(panel, out.at[pl.ds(0, rows)], sems.at[1])
    bring.start()
    copy.start()
    bring.wait()
    out[rows:, :] = digits(held[...])
    copy.wait()


def place(part, block, depth, first):
    reps = LANES // depth
    row = lax.broadcasted_iota(jnp.int32, (LANES, part.shape[1]), 0)
    inside = (row // depth) == first
    spread = []
    for p in range(2):
        rows = part[(2 * block + p) * depth:(2 * block + p + 1) * depth, :].astype(F32)
        spread.append(jnp.where(inside, jnp.concatenate([rows] * reps, axis=0), 0.0))
    upper = jnp.concatenate([spread[0], spread[1]], axis=1)
    lower = jnp.concatenate([-spread[1], spread[0]], axis=1)
    return jnp.concatenate([upper, lower], axis=0).astype(BF16)


def accumulate(slots, cols, tiles, shards, acc, weights):
    blocks = weights.shape[0]
    starts = []
    for s, (row, depth, parts) in enumerate(shards):
        reps = LANES // depth
        starts.append(pl.multiple_of(row // reps * LANES, LANES))
        share = blocks // len(parts)
        for b in range(blocks):
            weights[b, s * 2 * LANES:(s + 1) * 2 * LANES, :] = place(
                parts[b // share], b % share, depth, row % reps
            )
    for t in range(tiles.shape[0]):
        left = jnp.concatenate(
            [tiles[t, p, :, pl.ds(start, LANES)] for start in starts for p in range(2)], axis=1
        )
        acc[slots[t]] += jnp.dot(left, weights[cols[t]], preferred_element_type=F32)


def stage_kernel(slots, cols, own, tiles, slots_out, cols_out, own_out, out):
    del tiles
    slots_out[...] = slots[...]
    cols_out[...] = cols[...]
    own_out[...] = own[...]
    out[...] = jnp.zeros_like(out)


def hop_early(slots, cols, own, from_left, from_right, tiles, start, out, weights, *, n, depth):
    del start
    shards = [
        (shard_row(n, 0), depth, [own]),
        (shard_row(n, -1), depth, [from_left]),
        (shard_row(n, 1), depth, [from_right]),
    ]
    accumulate(slots, cols, tiles, shards, out, weights)


def hop_middle(slots, cols, from_left, from_right, tiles, start, out, weights, *, n, depth, hop):
    del start
    shards = [
        (shard_row(n, -hop), depth, [from_left]), (shard_row(n, hop), depth, [from_right])
    ]
    accumulate(slots, cols, tiles, shards, out, weights)


def hop_last(slots, cols, pole_weight, low, high, tiles, start, out, dens, weights, *, n, depth):
    del start
    accumulate(slots, cols, tiles, [(shard_row(n, n // 2), depth, [low, high])], out, weights)
    width = dens.shape[2]
    for slot in range(out.shape[0]):
        dens[slot] = -(pole_weight[0] * out[slot, :, width:] + pole_weight[1] * out[slot, :, :width])


def halves_kernel(acc, mine, other):
    col = lax.axis_index("col")
    half = mine.shape[2]
    width = mine.shape[3]
    for slot in range(acc.shape[0]):
        for p in range(2):
            cut = slice(p * width, (p + 1) * width)
            mine[slot, p] = -acc[slot, pl.ds(pl.multiple_of(col * half, half), half), cut]
            other[slot, p] = -acc[slot, pl.ds(pl.multiple_of((1 - col) * half, half), half), cut]


def earlier(total):
    first = lax.broadcasted_iota(jnp.int32, (total, total), 0)
    second = lax.broadcasted_iota(jnp.int32, (total, total), 1)
    return (first < second).astype(F32).astype(BF16)


def place_of(chip, n):
    apart = chip ^ lax.axis_index("row")
    top = (apart >= n // 2).astype(jnp.int32)
    step = jnp.where(top == 1, apart - n // 2, apart - 1)
    other = (top != lax.axis_index("col")).astype(jnp.int32)
    return jnp.where(apart == 0, 0, 1 + other * (n // 2) + step)


def basis_kernel(wanted, basis, supernode, out, wide, *, n, rows_chip, slots):
    wide[...] = supernode[...].astype(F32)
    boxes, orbitals, _ = basis.shape
    total = boxes * orbitals
    rows = wanted[...]
    asked = jnp.concatenate([rows[b:b + 1] for b in range(boxes)], axis=1)
    source = asked // rows_chip
    marks = (lax.broadcasted_iota(jnp.int32, (n, total), 0) == source).astype(F32)
    counts = jnp.dot(marks.astype(BF16), earlier(total), preferred_element_type=F32)
    rank = jnp.sum(marks * counts, axis=0, keepdims=True).astype(jnp.int32)
    slot = place_of(source, n) * slots + rank
    index = lax.broadcasted_iota(jnp.int32, (out.shape[1], orbitals), 0)
    for b in range(boxes):
        pick = (index == slot[:, b * orbitals:(b + 1) * orbitals]).astype(F32).astype(BF16)
        out[b] = jnp.dot(pick, basis[b], preferred_element_type=F32).astype(BF16)


def lines_kernel(*refs, n, hops, lines):
    *shards, out = refs
    for ref, hop in zip(shards, hops):
        at = pl.multiple_of(shard_row(n, hop) * lines, lines)
        out[pl.ds(at, lines), :] = ref[ref.shape[0] - lines:, :]


def pick_kernel(mine, theirs, out, *, n, lines, total, rows_chip, slots):
    row = lax.axis_index("row")
    col = lax.axis_index("col")
    first = jnp.where(col == 0, 1, n // 2)

    def asked_by(chip, own):
        at = pl.ds(pl.multiple_of(chip * lines, lines), lines)
        return undigits(jnp.where(own, mine[at, :].astype(F32), theirs[at, :].astype(F32)), total)

    asked = [asked_by(row, True)]
    for step in range(n // 2):
        chip = row ^ jnp.minimum(first + step, n - 1)
        asked += [asked_by(chip, col == 0), asked_by(chip, col == 1)]
    count = len(asked)
    asked = jnp.concatenate(asked, axis=0).astype(jnp.int32)
    here = (asked // rows_chip) == row
    local = (asked % rows_chip).astype(F32)
    rank = jnp.dot(
        here.astype(F32).astype(BF16), earlier(total), preferred_element_type=F32
    ).astype(jnp.int32)
    rank = jnp.where(here, rank, -1)
    index = lax.broadcasted_iota(jnp.int32, (slots, total), 0)
    lane = lax.broadcasted_iota(jnp.int32, (slots, rows_chip), 1)
    for d in range(count):
        chosen = jnp.where(index == rank[d:d + 1], local[d:d + 1], 0.0)
        at = jnp.sum(chosen, axis=1, keepdims=True).astype(jnp.int32)
        out[d * slots:(d + 1) * slots, :] = (lane == at).astype(F32).astype(BF16)


def add_kernel(mine, theirs, out):
    out[...] = mine[...] + theirs[...]


def select_kernel(pick, mine, theirs, *outs):
    rows = pick.shape[1]
    total = (mine[...] + theirs[...]).reshape(rows, mine.shape[2]).astype(BF16)
    rows_out = jnp.dot(pick[...], total, preferred_element_type=F32).astype(BF16)
    at = 0
    for out in outs:
        out[...] = rows_out[at:at + out.shape[0]]
        at += out.shape[0]


def turn_kernel(*refs):
    *parts, out = refs
    slots = out.shape[0] // len(parts)
    at = pl.ds(pl.multiple_of((1 - lax.axis_index("col")) * slots, slots), slots)
    for i, part in enumerate(parts):
        out[i * slots:(i + 1) * slots] = part[at, :]


def density_kernel(*refs):
    own, *parts, passed, basis, supernode, out = refs
    slots = own.shape[0]
    at = pl.ds(pl.multiple_of(lax.axis_index("col") * slots, slots), slots)
    arrived = jnp.concatenate(
        [own[...]] + [part[at, :] for part in parts] + [passed[...]], axis=0
    )
    for n in range(basis.shape[0]):
        projected = lax.dot_general(
            arrived, basis[n], (((0,), (0,)), ((), ())), preferred_element_type=F32
        )
        out[n:n + 1, :] = jnp.sum(supernode[n] * projected, axis=0, keepdims=True)


def local(n_row, panel, tiles, tile_slot, tile_col, pole_weight, box_orbitals, box_basis, supernode_basis):
    order = ring_order(n_row)
    half_ring = n_row // 2
    to_right = [(order[i], order[(i + 1) % n_row]) for i in range(n_row)]
    to_left = [(order[(i + 1) % n_row], order[i]) for i in range(n_row)]
    _, blocks, parts, depth, width = panel.shape
    tile_count, _, order_b, _ = tiles.shape
    boxes, orbitals = box_orbitals.shape
    total = boxes * orbitals
    rows_chip = BR_DEV * order_b
    slots = 2 * total // n_row
    arrive = (1 + 2 * half_ring) * slots
    half = order_b // 2
    shard_rows = blocks * parts * depth
    lines = -(-2 * total // (16 * LANES)) * 16
    acc_shape = (BR_DEV, order_b, 2 * width)
    acc_out = jax.ShapeDtypeStruct(acc_shape, F32)
    in_vmem = pl.BlockSpec(memory_space=pltpu.VMEM)
    in_smem = pl.BlockSpec(memory_space=pltpu.SMEM)
    in_hbm = pl.BlockSpec(memory_space=pltpu.HBM)
    params = pltpu.CompilerParams(vmem_limit_bytes=VMEM_LIMIT)
    cost = pl.CostEstimate(flops=2 ** 20, bytes_accessed=2 ** 20, transcendentals=0)

    def call(body, in_specs, out_shape, before, shards, aliases={}):
        weights = pltpu.VMEM((blocks, shards * 2 * LANES, 2 * width), BF16)
        return pl.pallas_call(
            functools.partial(body, n=n_row, depth=depth),
            in_specs=in_specs,
            out_specs=jax.tree.map(lambda _: in_vmem, out_shape),
            out_shape=out_shape,
            scratch_shapes=[*before, weights],
            input_output_aliases=aliases,
            compiler_params=params,
            cost_estimate=cost,
        )

    own = pl.pallas_call(
        pack_kernel,
        in_specs=[in_hbm, in_hbm],
        out_specs=in_vmem,
        out_shape=jax.ShapeDtypeStruct((shard_rows + lines, width), BF16),
        scratch_shapes=[pltpu.VMEM(box_orbitals.shape, jnp.int32), pltpu.SemaphoreType.DMA((2,))],
        compiler_params=pltpu.CompilerParams(vmem_limit_bytes=PACK_LIMIT),
        cost_estimate=cost,
    )(panel.reshape(shard_rows, width), box_orbitals)

    basis_here, wide = pl.pallas_call(
        functools.partial(basis_kernel, n=n_row, rows_chip=rows_chip, slots=slots),
        out_shape=[
            jax.ShapeDtypeStruct((boxes, arrive, box_basis.shape[2]), BF16),
            jax.ShapeDtypeStruct(supernode_basis.shape, F32),
        ],
        compiler_params=params,
        cost_estimate=cost,
    )(box_orbitals, box_basis, supernode_basis)

    left, right = own, own
    seen, hops = [own], [0]
    acc = None
    for h in range(1, half_ring + 1):
        if h < half_ring:
            next_left = lax.ppermute(left, "row", to_right)
            next_right = lax.ppermute(right, "row", to_left)
        else:
            cut = shard_rows // 2
            next_left = lax.ppermute(left[:cut], "row", to_right)
            next_right = lax.ppermute(right[cut:], "row", to_left)
        if h == 1:
            tile_slot, tile_col, own, acc = pl.pallas_call(
                stage_kernel,
                in_specs=[in_vmem] * 4,
                out_specs=[in_vmem] * 4,
                out_shape=[
                    jax.ShapeDtypeStruct(tile_slot.shape, jnp.int32),
                    jax.ShapeDtypeStruct(tile_col.shape, jnp.int32),
                    jax.ShapeDtypeStruct(own.shape, BF16),
                    acc_out,
                ],
                compiler_params=params,
                cost_estimate=cost,
            )(tile_slot, tile_col, own, tiles)
            seen[0] = own
        elif h == 2:
            acc = call(
                hop_early, [in_smem] * 2 + [in_vmem] * 5, acc_out, [], 3, aliases={6: 0}
            )(tile_slot, tile_col, own, left, right, tiles, acc)
        elif h > 2:
            acc = call(
                functools.partial(hop_middle, hop=h - 1),
                [in_smem] * 2 + [in_vmem] * 4,
                acc_out,
                [],
                2,
                aliases={5: 0},
            )(tile_slot, tile_col, left, right, tiles, acc)
        if h == half_ring - 1:
            next_left, basis_here, wide = lax.optimization_barrier((next_left, basis_here, wide))
        left, done = lax.optimization_barrier((next_left, acc))
        right, _ = lax.optimization_barrier((next_right, acc))
        acc = done
        if h < half_ring:
            seen += [left, right]
            hops += [-h, h]
        else:
            seen.append(right)
            hops.append(h)

    swap = [(0, 1), (1, 0)]
    wanted = pl.pallas_call(
        functools.partial(lines_kernel, n=n_row, hops=hops, lines=lines),
        out_shape=jax.ShapeDtypeStruct((n_row * lines, width), BF16),
        compiler_params=params,
        cost_estimate=cost,
    )(*seen)
    left, wanted = lax.optimization_barrier((left, wanted))
    wanted_other = lax.ppermute(wanted, "col", swap)

    half_shape = (BR_DEV, 2, half, width)
    acc, dens = call(
        hop_last,
        [in_smem] * 3 + [in_vmem] * 4,
        [acc_out, jax.ShapeDtypeStruct((BR_DEV, order_b, width), F32)],
        [],
        1,
        aliases={6: 0},
    )(tile_slot, tile_col, pole_weight, left, right, tiles, acc)
    dens, wanted_other = lax.optimization_barrier((dens, wanted_other))
    dens_other = lax.ppermute(dens, "col", swap)
    pick = pl.pallas_call(
        functools.partial(
            pick_kernel, n=n_row, lines=lines, total=total, rows_chip=rows_chip, slots=slots
        ),
        out_shape=jax.ShapeDtypeStruct((arrive, rows_chip), BF16),
        compiler_params=params,
        cost_estimate=pl.CostEstimate(flops=2 ** 32, bytes_accessed=2 ** 20, transcendentals=0),
    )(wanted, wanted_other)
    message = jax.ShapeDtypeStruct((2 * slots, width), BF16)
    kept, *sent = pl.pallas_call(
        select_kernel,
        out_shape=[jax.ShapeDtypeStruct((slots, width), BF16)] + [message] * half_ring,
        compiler_params=params,
        cost_estimate=cost,
    )(pick, dens, dens_other)

    fetched = []
    for step in range(half_ring):
        pairs = [(2 * r + 1, 2 * (r ^ (half_ring + step)) + 1) for r in range(n_row)]
        if step + 1 < half_ring:
            pairs += [(2 * r, 2 * (r ^ (1 + step))) for r in range(n_row)]
        fetched.append(lax.ppermute(sent[step], ("row", "col"), pairs))

    turned = pl.pallas_call(
        turn_kernel,
        out_shape=jax.ShapeDtypeStruct((half_ring * slots, width), BF16),
        compiler_params=params,
        cost_estimate=cost,
    )(*fetched)
    passed = lax.ppermute(turned, "col", swap)

    mine, other = pl.pallas_call(
        halves_kernel,
        out_shape=[jax.ShapeDtypeStruct(half_shape, F32)] * 2,
        compiler_params=params,
        cost_estimate=cost,
    )(acc)
    inverse_other = lax.ppermute(other, "col", swap)
    inverse = pl.pallas_call(
        add_kernel,
        out_shape=jax.ShapeDtypeStruct(half_shape, F32),
        compiler_params=params,
        cost_estimate=cost,
    )(mine, inverse_other)
    kept, inverse = lax.optimization_barrier((kept, inverse))
    density = pl.pallas_call(
        density_kernel,
        out_shape=jax.ShapeDtypeStruct((boxes, box_basis.shape[2]), F32),
        compiler_params=params,
    )(kept, *fetched, passed, basis_here, wide)
    return inverse, density


def solution(mesh):
    return jax.shard_map(
        functools.partial(local, mesh.shape["row"]),
        mesh=mesh,
        in_specs=(
            P(("pole", "col"), None, None, "row", None),
            P(("pole", "row", "col"), None, None, None),
            P(("pole", "row", "col")),
            P(("pole", "row", "col")),
            P("pole"),
            P(("pole", "row", "col"), None),
            P(("pole", "row", "col"), None, None),
            P(("pole", "row", "col"), None, None),
        ),
        out_specs=(P(("pole", "row"), None, "col", None), P(("pole", "row", "col"), None)),
        check_vma=False,
    )
```

```python
import functools

import jax
import jax.numpy as jnp
from jax import lax
from jax.experimental import pallas as pl
from jax.experimental.pallas import tpu as pltpu
from jax.sharding import PartitionSpec as P

BR_DEV = 2
LANES = 128
F32 = jnp.float32
BF16 = jnp.bfloat16
VMEM_LIMIT = 8 * 1024 * 1024
PACK_LIMIT = 8 * 1024 * 1024


def ring_order(n):
    if n <= 8 and n % 2 == 0:
        return list(range(0, n, 2)) + list(range(n - 1, 0, -2))
    return list(range(n))


def shard_row(n, hop):
    row = lax.axis_index("row")
    if ring_order(n) == list(range(n)):
        return lax.rem(row + hop + n, n)
    at = jnp.where(row % 2 == 0, row // 2, n - 1 - row // 2)
    at = lax.rem(at + hop + n, n)
    return jnp.where(at < n // 2, 2 * at, 2 * (n - 1 - at) + 1)


def digits(rows):
    boxes, orbitals = rows.shape
    pieces = [rows[n:n + 1, c:c + LANES] for n in range(boxes) for c in range(0, orbitals, LANES)]
    lines = [piece // 256 for piece in pieces] + [piece % 256 for piece in pieces]
    pad = -len(lines) % 16
    lines.append(jnp.zeros((pad, LANES), jnp.int32))
    return jnp.concatenate(lines, axis=0).astype(F32).astype(BF16)


def undigits(lines, total):
    count = total // LANES
    lines = lines.astype(F32)
    whole = lines[:count] * 256.0 + lines[count:2 * count]
    return jnp.concatenate([whole[i:i + 1] for i in range(count)], axis=1)


def pack_kernel(panel, wanted, out, held, sems):
    rows = panel.shape[0]
    bring = pltpu.make_async_copy(wanted, held, sems.at[0])
    copy = pltpu.make_async_copy(panel, out.at[pl.ds(0, rows)], sems.at[1])
    bring.start()
    copy.start()
    bring.wait()
    out[rows:, :] = digits(held[...])
    copy.wait()


def place(part, block, depth, first):
    reps = LANES // depth
    row = lax.broadcasted_iota(jnp.int32, (LANES, part.shape[1]), 0)
    inside = (row // depth) == first
    spread = []
    for p in range(2):
        rows = part[(2 * block + p) * depth:(2 * block + p + 1) * depth, :].astype(F32)
        spread.append(jnp.where(inside, jnp.concatenate([rows] * reps, axis=0), 0.0))
    upper = jnp.concatenate([spread[0], spread[1]], axis=1)
    lower = jnp.concatenate([-spread[1], spread[0]], axis=1)
    return jnp.concatenate([upper, lower], axis=0).astype(BF16)


def accumulate(slots, cols, tiles, shards, acc, weights):
    blocks = weights.shape[0]
    starts = []
    for s, (row, depth, parts) in enumerate(shards):
        reps = LANES // depth
        starts.append(pl.multiple_of(row // reps * LANES, LANES))
        share = blocks // len(parts)
        for b in range(blocks):
            weights[b, s * 2 * LANES:(s + 1) * 2 * LANES, :] = place(
                parts[b // share], b % share, depth, row % reps
            )
    for t in range(tiles.shape[0]):
        left = jnp.concatenate(
            [tiles[t, p, :, pl.ds(start, LANES)] for start in starts for p in range(2)], axis=1
        )
        acc[slots[t]] += jnp.dot(left, weights[cols[t]], preferred_element_type=F32)


def stage_kernel(slots, cols, own, tiles, slots_out, cols_out, own_out, out):
    del tiles
    slots_out[...] = slots[...]
    cols_out[...] = cols[...]
    own_out[...] = own[...]
    out[...] = jnp.zeros_like(out)


def hop_early(slots, cols, own, from_left, from_right, tiles, start, out, weights, *, n, depth):
    del start
    shards = [
        (shard_row(n, 0), depth, [own]),
        (shard_row(n, -1), depth, [from_left]),
        (shard_row(n, 1), depth, [from_right]),
    ]
    accumulate(slots, cols, tiles, shards, out, weights)


def hop_middle(slots, cols, from_left, from_right, tiles, start, out, weights, *, n, depth, hop):
    del start
    shards = [
        (shard_row(n, -hop), depth, [from_left]), (shard_row(n, hop), depth, [from_right])
    ]
    accumulate(slots, cols, tiles, shards, out, weights)


def hop_last(slots, cols, pole_weight, low, high, tiles, start, out, dens, weights, *, n, depth):
    del start
    accumulate(slots, cols, tiles, [(shard_row(n, n // 2), depth, [low, high])], out, weights)
    width = dens.shape[2]
    for slot in range(out.shape[0]):
        dens[slot] = -(pole_weight[0] * out[slot, :, width:] + pole_weight[1] * out[slot, :, :width])


def halves_kernel(acc, mine, other):
    col = lax.axis_index("col")
    half = mine.shape[2]
    width = mine.shape[3]
    for slot in range(acc.shape[0]):
        for p in range(2):
            cut = slice(p * width, (p + 1) * width)
            mine[slot, p] = -acc[slot, pl.ds(pl.multiple_of(col * half, half), half), cut]
            other[slot, p] = -acc[slot, pl.ds(pl.multiple_of((1 - col) * half, half), half), cut]


def earlier(total):
    first = lax.broadcasted_iota(jnp.int32, (total, total), 0)
    second = lax.broadcasted_iota(jnp.int32, (total, total), 1)
    return (first < second).astype(F32).astype(BF16)


def peers(n):
    half = n // 2
    return list(range(n - 1, half + 1, -1)) + [half], list(range(1, half)) + [half + 1]


def place_of(chip, n):
    apart = chip ^ lax.axis_index("row")
    place = jnp.zeros_like(apart)
    for core, steps in enumerate(peers(n)):
        first = jnp.where(lax.axis_index("col") == core, 1, 1 + n // 2)
        for step, k in enumerate(steps):
            place = jnp.where(apart == k, first + step, place)
    return place


def basis_kernel(wanted, basis, supernode, out, wide, *, n, rows_chip, slots):
    wide[...] = supernode[...].astype(F32)
    boxes, orbitals, _ = basis.shape
    total = boxes * orbitals
    rows = wanted[...]
    asked = jnp.concatenate([rows[b:b + 1] for b in range(boxes)], axis=1)
    source = asked // rows_chip
    marks = (lax.broadcasted_iota(jnp.int32, (n, total), 0) == source).astype(F32)
    counts = jnp.dot(marks.astype(BF16), earlier(total), preferred_element_type=F32)
    rank = jnp.sum(marks * counts, axis=0, keepdims=True).astype(jnp.int32)
    slot = place_of(source, n) * slots + rank
    index = lax.broadcasted_iota(jnp.int32, (out.shape[1], orbitals), 0)
    for b in range(boxes):
        pick = (index == slot[:, b * orbitals:(b + 1) * orbitals]).astype(F32).astype(BF16)
        out[b] = jnp.dot(pick, basis[b], preferred_element_type=F32).astype(BF16)


def lines_kernel(*refs, n, hops, lines):
    *shards, out = refs
    for ref, hop in zip(shards, hops):
        at = pl.multiple_of(shard_row(n, hop) * lines, lines)
        out[pl.ds(at, lines), :] = ref[ref.shape[0] - lines:, :]


def pick_kernel(mine, theirs, out, *, n, lines, total, rows_chip, slots):
    row = lax.axis_index("row")
    col = lax.axis_index("col")
    far, near = peers(n)
    far = far + near[-1:]

    def asked_by(chip, own):
        at = pl.ds(pl.multiple_of(chip * lines, lines), lines)
        return undigits(jnp.where(own, mine[at, :].astype(F32), theirs[at, :].astype(F32)), total)

    asked = [asked_by(row, True)]
    for step in range(n // 2):
        chip = row ^ jnp.where(col == 0, far[step], near[step])
        asked += [asked_by(chip, col == 0), asked_by(chip, col == 1)]
    count = len(asked)
    asked = jnp.concatenate(asked, axis=0).astype(jnp.int32)
    here = (asked // rows_chip) == row
    local = (asked % rows_chip).astype(F32)
    rank = jnp.dot(
        here.astype(F32).astype(BF16), earlier(total), preferred_element_type=F32
    ).astype(jnp.int32)
    rank = jnp.where(here, rank, -1)
    index = lax.broadcasted_iota(jnp.int32, (slots, total), 0)
    lane = lax.broadcasted_iota(jnp.int32, (slots, rows_chip), 1)
    for d in range(count):
        chosen = jnp.where(index == rank[d:d + 1], local[d:d + 1], 0.0)
        at = jnp.sum(chosen, axis=1, keepdims=True).astype(jnp.int32)
        out[d * slots:(d + 1) * slots, :] = (lane == at).astype(F32).astype(BF16)


def add_kernel(mine, theirs, out):
    out[...] = mine[...] + theirs[...]


def select_kernel(pick, mine, theirs, *outs):
    rows = pick.shape[1]
    total = (mine[...] + theirs[...]).reshape(rows, mine.shape[2]).astype(BF16)
    rows_out = jnp.dot(pick[...], total, preferred_element_type=F32).astype(BF16)
    at = 0
    for out in outs:
        out[...] = rows_out[at:at + out.shape[0]]
        at += out.shape[0]


def turn_kernel(*refs):
    *parts, out = refs
    slots = out.shape[0] // len(parts)
    at = pl.ds(pl.multiple_of((1 - lax.axis_index("col")) * slots, slots), slots)
    for i, part in enumerate(parts):
        out[i * slots:(i + 1) * slots] = part[at, :]


def density_kernel(*refs):
    own, *parts, passed, basis, supernode, out = refs
    slots = own.shape[0]
    at = pl.ds(pl.multiple_of(lax.axis_index("col") * slots, slots), slots)
    arrived = jnp.concatenate(
        [own[...]] + [part[at, :] for part in parts] + [passed[...]], axis=0
    )
    for n in range(basis.shape[0]):
        projected = lax.dot_general(
            arrived, basis[n], (((0,), (0,)), ((), ())), preferred_element_type=F32
        )
        out[n:n + 1, :] = jnp.sum(supernode[n] * projected, axis=0, keepdims=True)


def local(n_row, panel, tiles, tile_slot, tile_col, pole_weight, box_orbitals, box_basis, supernode_basis):
    order = ring_order(n_row)
    half_ring = n_row // 2
    to_right = [(order[i], order[(i + 1) % n_row]) for i in range(n_row)]
    to_left = [(order[(i + 1) % n_row], order[i]) for i in range(n_row)]
    _, blocks, parts, depth, width = panel.shape
    tile_count, _, order_b, _ = tiles.shape
    boxes, orbitals = box_orbitals.shape
    total = boxes * orbitals
    rows_chip = BR_DEV * order_b
    slots = 2 * total // n_row
    arrive = (1 + 2 * half_ring) * slots
    half = order_b // 2
    shard_rows = blocks * parts * depth
    lines = -(-2 * total // (16 * LANES)) * 16
    acc_shape = (BR_DEV, order_b, 2 * width)
    acc_out = jax.ShapeDtypeStruct(acc_shape, F32)
    in_vmem = pl.BlockSpec(memory_space=pltpu.VMEM)
    in_smem = pl.BlockSpec(memory_space=pltpu.SMEM)
    in_hbm = pl.BlockSpec(memory_space=pltpu.HBM)
    params = pltpu.CompilerParams(vmem_limit_bytes=VMEM_LIMIT)
    cost = pl.CostEstimate(flops=2 ** 20, bytes_accessed=2 ** 20, transcendentals=0)

    def call(body, in_specs, out_shape, before, shards, aliases={}):
        weights = pltpu.VMEM((blocks, shards * 2 * LANES, 2 * width), BF16)
        return pl.pallas_call(
            functools.partial(body, n=n_row, depth=depth),
            in_specs=in_specs,
            out_specs=jax.tree.map(lambda _: in_vmem, out_shape),
            out_shape=out_shape,
            scratch_shapes=[*before, weights],
            input_output_aliases=aliases,
            compiler_params=params,
            cost_estimate=cost,
        )

    own = pl.pallas_call(
        pack_kernel,
        in_specs=[in_hbm, in_hbm],
        out_specs=in_vmem,
        out_shape=jax.ShapeDtypeStruct((shard_rows + lines, width), BF16),
        scratch_shapes=[pltpu.VMEM(box_orbitals.shape, jnp.int32), pltpu.SemaphoreType.DMA((2,))],
        compiler_params=pltpu.CompilerParams(vmem_limit_bytes=PACK_LIMIT),
        cost_estimate=cost,
    )(panel.reshape(shard_rows, width), box_orbitals)

    basis_here, wide = pl.pallas_call(
        functools.partial(basis_kernel, n=n_row, rows_chip=rows_chip, slots=slots),
        out_shape=[
            jax.ShapeDtypeStruct((boxes, arrive, box_basis.shape[2]), BF16),
            jax.ShapeDtypeStruct(supernode_basis.shape, F32),
        ],
        compiler_params=params,
        cost_estimate=cost,
    )(box_orbitals, box_basis, supernode_basis)

    left, right = own, own
    seen, hops = [own], [0]
    acc = None
    for h in range(1, half_ring + 1):
        if h < half_ring:
            next_left = lax.ppermute(left, "row", to_right)
            next_right = lax.ppermute(right, "row", to_left)
        else:
            cut = shard_rows // 2
            next_left = lax.ppermute(left[:cut], "row", to_right)
            next_right = lax.ppermute(right[cut:], "row", to_left)
        if h == 1:
            tile_slot, tile_col, own, acc = pl.pallas_call(
                stage_kernel,
                in_specs=[in_vmem] * 4,
                out_specs=[in_vmem] * 4,
                out_shape=[
                    jax.ShapeDtypeStruct(tile_slot.shape, jnp.int32),
                    jax.ShapeDtypeStruct(tile_col.shape, jnp.int32),
                    jax.ShapeDtypeStruct(own.shape, BF16),
                    acc_out,
                ],
                compiler_params=params,
                cost_estimate=cost,
            )(tile_slot, tile_col, own, tiles)
            seen[0] = own
        elif h == 2:
            acc = call(
                hop_early, [in_smem] * 2 + [in_vmem] * 5, acc_out, [], 3, aliases={6: 0}
            )(tile_slot, tile_col, own, left, right, tiles, acc)
        elif h > 2:
            acc = call(
                functools.partial(hop_middle, hop=h - 1),
                [in_smem] * 2 + [in_vmem] * 4,
                acc_out,
                [],
                2,
                aliases={5: 0},
            )(tile_slot, tile_col, left, right, tiles, acc)
        if h == half_ring - 1:
            next_left, basis_here, wide = lax.optimization_barrier((next_left, basis_here, wide))
        left, done = lax.optimization_barrier((next_left, acc))
        right, _ = lax.optimization_barrier((next_right, acc))
        acc = done
        if h < half_ring:
            seen += [left, right]
            hops += [-h, h]
        else:
            seen.append(right)
            hops.append(h)

    swap = [(0, 1), (1, 0)]
    wanted = pl.pallas_call(
        functools.partial(lines_kernel, n=n_row, hops=hops, lines=lines),
        out_shape=jax.ShapeDtypeStruct((n_row * lines, width), BF16),
        compiler_params=params,
        cost_estimate=cost,
    )(*seen)
    left, wanted = lax.optimization_barrier((left, wanted))
    wanted_other = lax.ppermute(wanted, "col", swap)

    half_shape = (BR_DEV, 2, half, width)
    acc, dens = call(
        hop_last,
        [in_smem] * 3 + [in_vmem] * 4,
        [acc_out, jax.ShapeDtypeStruct((BR_DEV, order_b, width), F32)],
        [],
        1,
        aliases={6: 0},
    )(tile_slot, tile_col, pole_weight, left, right, tiles, acc)
    dens, wanted_other = lax.optimization_barrier((dens, wanted_other))
    dens_other = lax.ppermute(dens, "col", swap)
    pick = pl.pallas_call(
        functools.partial(
            pick_kernel, n=n_row, lines=lines, total=total, rows_chip=rows_chip, slots=slots
        ),
        out_shape=jax.ShapeDtypeStruct((arrive, rows_chip), BF16),
        compiler_params=params,
        cost_estimate=pl.CostEstimate(flops=2 ** 32, bytes_accessed=2 ** 20, transcendentals=0),
    )(wanted, wanted_other)
    message = jax.ShapeDtypeStruct((2 * slots, width), BF16)
    kept, *sent = pl.pallas_call(
        select_kernel,
        out_shape=[jax.ShapeDtypeStruct((slots, width), BF16)] + [message] * half_ring,
        compiler_params=params,
        cost_estimate=cost,
    )(pick, dens, dens_other)

    far, near = peers(n_row)
    fetched = []
    for step in range(half_ring):
        pairs = [(2 * r + 1, 2 * (r ^ near[step]) + 1) for r in range(n_row)]
        if step < len(far):
            pairs += [(2 * r, 2 * (r ^ far[step])) for r in range(n_row)]
        fetched.append(lax.ppermute(sent[step], ("row", "col"), pairs))

    turned = pl.pallas_call(
        turn_kernel,
        out_shape=jax.ShapeDtypeStruct((half_ring * slots, width), BF16),
        compiler_params=params,
        cost_estimate=cost,
    )(*fetched)
    passed = lax.ppermute(turned, "col", swap)

    mine, other = pl.pallas_call(
        halves_kernel,
        out_shape=[jax.ShapeDtypeStruct(half_shape, F32)] * 2,
        compiler_params=params,
        cost_estimate=cost,
    )(acc)
    inverse_other = lax.ppermute(other, "col", swap)
    inverse = pl.pallas_call(
        add_kernel,
        out_shape=jax.ShapeDtypeStruct(half_shape, F32),
        compiler_params=params,
        cost_estimate=cost,
    )(mine, inverse_other)
    kept, inverse = lax.optimization_barrier((kept, inverse))
    density = pl.pallas_call(
        density_kernel,
        out_shape=jax.ShapeDtypeStruct((boxes, box_basis.shape[2]), F32),
        compiler_params=params,
    )(kept, *fetched, passed, basis_here, wide)
    return inverse, density


def solution(mesh):
    return jax.shard_map(
        functools.partial(local, mesh.shape["row"]),
        mesh=mesh,
        in_specs=(
            P(("pole", "col"), None, None, "row", None),
            P(("pole", "row", "col"), None, None, None),
            P(("pole", "row", "col")),
            P(("pole", "row", "col")),
            P("pole"),
            P(("pole", "row", "col"), None),
            P(("pole", "row", "col"), None, None),
            P(("pole", "row", "col"), None, None),
        ),
        out_specs=(P(("pole", "row"), None, "col", None), P(("pole", "row", "col"), None)),
        check_vma=False,
    )
```

```python
import functools

import jax
import jax.numpy as jnp
from jax import lax
from jax.experimental import pallas as pl
from jax.experimental.pallas import tpu as pltpu
from jax.sharding import PartitionSpec as P

BR_DEV = 2
LANES = 128
F32 = jnp.float32
BF16 = jnp.bfloat16
VMEM_LIMIT = 8 * 1024 * 1024


def ring_order(n):
    if n <= 8 and n % 2 == 0:
        return list(range(0, n, 2)) + list(range(n - 1, 0, -2))
    return list(range(n))


def shard_row(n, hop):
    row = lax.axis_index("row")
    if ring_order(n) == list(range(n)):
        return lax.rem(row + hop + n, n)
    at = jnp.where(row % 2 == 0, row // 2, n - 1 - row // 2)
    at = lax.rem(at + hop + n, n)
    return jnp.where(at < n // 2, 2 * at, 2 * (n - 1 - at) + 1)


def digits(rows):
    boxes, orbitals = rows.shape
    pieces = [rows[n:n + 1, c:c + LANES] for n in range(boxes) for c in range(0, orbitals, LANES)]
    lines = [piece // 256 for piece in pieces] + [piece % 256 for piece in pieces]
    pad = -len(lines) % 16
    lines.append(jnp.zeros((pad, LANES), jnp.int32))
    return jnp.concatenate(lines, axis=0).astype(F32).astype(BF16)


def undigits(lines, total):
    count = total // LANES
    lines = lines.astype(F32)
    whole = lines[:count] * 256.0 + lines[count:2 * count]
    return jnp.concatenate([whole[i:i + 1] for i in range(count)], axis=1)


def digits_kernel(wanted, out):
    out[...] = digits(wanted[...])


def pack_kernel(rows, lines, out):
    out[:rows.shape[0], :] = rows[...]
    out[rows.shape[0]:, :] = lines[...]


def place(part, block, depth, first):
    reps = LANES // depth
    row = lax.broadcasted_iota(jnp.int32, (LANES, part.shape[1]), 0)
    inside = (row // depth) == first
    spread = []
    for p in range(2):
        rows = part[(2 * block + p) * depth:(2 * block + p + 1) * depth, :].astype(F32)
        spread.append(jnp.where(inside, jnp.concatenate([rows] * reps, axis=0), 0.0))
    upper = jnp.concatenate([spread[0], spread[1]], axis=1)
    lower = jnp.concatenate([-spread[1], spread[0]], axis=1)
    return jnp.concatenate([upper, lower], axis=0).astype(BF16)


def accumulate(slots, cols, tiles, shards, acc, weights):
    blocks = weights.shape[0]
    starts = []
    for s, (row, depth, parts) in enumerate(shards):
        reps = LANES // depth
        starts.append(pl.multiple_of(row // reps * LANES, LANES))
        share = blocks // len(parts)
        for b in range(blocks):
            weights[b, s * 2 * LANES:(s + 1) * 2 * LANES, :] = place(
                parts[b // share], b % share, depth, row % reps
            )
    for t in range(tiles.shape[0]):
        left = jnp.concatenate(
            [tiles[t, p, :, pl.ds(start, LANES)] for start in starts for p in range(2)], axis=1
        )
        acc[slots[t]] += jnp.dot(left, weights[cols[t]], preferred_element_type=F32)


def hop_early(slots, cols, own, from_left, from_right, tiles, out, weights, *, n, depth):
    out[...] = jnp.zeros_like(out)
    shards = [
        (shard_row(n, 0), depth, [own]),
        (shard_row(n, -1), depth, [from_left]),
        (shard_row(n, 1), depth, [from_right]),
    ]
    accumulate(slots, cols, tiles, shards, out, weights)


def hop_middle(slots, cols, from_left, from_right, tiles, start, out, weights, *, n, depth, hop):
    del start
    shards = [
        (shard_row(n, -hop), depth, [from_left]), (shard_row(n, hop), depth, [from_right])
    ]
    accumulate(slots, cols, tiles, shards, out, weights)


def hop_last(slots, cols, pole_weight, low, high, tiles, start, out, dens, weights, *, n, depth):
    del start
    accumulate(slots, cols, tiles, [(shard_row(n, n // 2), depth, [low, high])], out, weights)
    width = dens.shape[2]
    for slot in range(out.shape[0]):
        dens[slot] = -(pole_weight[0] * out[slot, :, width:] + pole_weight[1] * out[slot, :, :width])


def halves_kernel(acc, mine, other):
    col = lax.axis_index("col")
    half = mine.shape[2]
    width = mine.shape[3]
    for slot in range(acc.shape[0]):
        for p in range(2):
            cut = slice(p * width, (p + 1) * width)
            mine[slot, p] = -acc[slot, pl.ds(pl.multiple_of(col * half, half), half), cut]
            other[slot, p] = -acc[slot, pl.ds(pl.multiple_of((1 - col) * half, half), half), cut]


def earlier(total):
    first = lax.broadcasted_iota(jnp.int32, (total, total), 0)
    second = lax.broadcasted_iota(jnp.int32, (total, total), 1)
    return (first < second).astype(F32).astype(BF16)


def peers(n):
    half = n // 2
    return list(range(n - 1, half + 1, -1)) + [half], list(range(1, half)) + [half + 1]


def place_of(chip, n):
    apart = chip ^ lax.axis_index("row")
    place = jnp.zeros_like(apart)
    for core, steps in enumerate(peers(n)):
        first = jnp.where(lax.axis_index("col") == core, 1, 1 + n // 2)
        for step, k in enumerate(steps):
            place = jnp.where(apart == k, first + step, place)
    return place


def basis_kernel(wanted, basis, supernode, out, wide, *, n, rows_chip, slots):
    wide[...] = supernode[...].astype(F32)
    boxes, orbitals, _ = basis.shape
    total = boxes * orbitals
    rows = wanted[...]
    asked = jnp.concatenate([rows[b:b + 1] for b in range(boxes)], axis=1)
    source = asked // rows_chip
    marks = (lax.broadcasted_iota(jnp.int32, (n, total), 0) == source).astype(F32)
    counts = jnp.dot(marks.astype(BF16), earlier(total), preferred_element_type=F32)
    rank = jnp.sum(marks * counts, axis=0, keepdims=True).astype(jnp.int32)
    slot = place_of(source, n) * slots + rank
    index = lax.broadcasted_iota(jnp.int32, (out.shape[1], orbitals), 0)
    for b in range(boxes):
        pick = (index == slot[:, b * orbitals:(b + 1) * orbitals]).astype(F32).astype(BF16)
        out[b] = jnp.dot(pick, basis[b], preferred_element_type=F32).astype(BF16)


def lines_kernel(*refs, n, hops, lines):
    *shards, out = refs
    for ref, hop in zip(shards, hops):
        at = pl.multiple_of(shard_row(n, hop) * lines, lines)
        out[pl.ds(at, lines), :] = ref[ref.shape[0] - lines:, :]


def pick_kernel(mine, theirs, out, *, n, lines, total, rows_chip, slots):
    row = lax.axis_index("row")
    col = lax.axis_index("col")
    far, near = peers(n)
    far = far + near[-1:]

    def asked_by(chip, own):
        at = pl.ds(pl.multiple_of(chip * lines, lines), lines)
        return undigits(jnp.where(own, mine[at, :].astype(F32), theirs[at, :].astype(F32)), total)

    asked = [asked_by(row, True)]
    for step in range(n // 2):
        chip = row ^ jnp.where(col == 0, far[step], near[step])
        asked += [asked_by(chip, col == 0), asked_by(chip, col == 1)]
    count = len(asked)
    asked = jnp.concatenate(asked, axis=0).astype(jnp.int32)
    here = (asked // rows_chip) == row
    local = (asked % rows_chip).astype(F32)
    rank = jnp.dot(
        here.astype(F32).astype(BF16), earlier(total), preferred_element_type=F32
    ).astype(jnp.int32)
    rank = jnp.where(here, rank, -1)
    index = lax.broadcasted_iota(jnp.int32, (slots, total), 0)
    lane = lax.broadcasted_iota(jnp.int32, (slots, rows_chip), 1)
    for d in range(count):
        chosen = jnp.where(index == rank[d:d + 1], local[d:d + 1], 0.0)
        at = jnp.sum(chosen, axis=1, keepdims=True).astype(jnp.int32)
        out[d * slots:(d + 1) * slots, :] = (lane == at).astype(F32).astype(BF16)


def add_kernel(mine, theirs, out):
    out[...] = mine[...] + theirs[...]


def select_kernel(pick, mine, theirs, *outs):
    rows = pick.shape[1]
    total = (mine[...] + theirs[...]).reshape(rows, mine.shape[2]).astype(BF16)
    rows_out = jnp.dot(pick[...], total, preferred_element_type=F32).astype(BF16)
    at = 0
    for out in outs:
        out[...] = rows_out[at:at + out.shape[0]]
        at += out.shape[0]


def turn_kernel(*refs):
    *parts, out = refs
    slots = out.shape[0] // len(parts)
    at = pl.ds(pl.multiple_of((1 - lax.axis_index("col")) * slots, slots), slots)
    for i, part in enumerate(parts):
        out[i * slots:(i + 1) * slots] = part[at, :]


def density_kernel(*refs):
    own, *parts, passed, basis, supernode, out = refs
    slots = own.shape[0]
    at = pl.ds(pl.multiple_of(lax.axis_index("col") * slots, slots), slots)
    arrived = jnp.concatenate(
        [own[...]] + [part[at, :] for part in parts] + [passed[...]], axis=0
    )
    for n in range(basis.shape[0]):
        projected = lax.dot_general(
            arrived, basis[n], (((0,), (0,)), ((), ())), preferred_element_type=F32
        )
        out[n:n + 1, :] = jnp.sum(supernode[n] * projected, axis=0, keepdims=True)


def local(n_row, panel, tiles, tile_slot, tile_col, pole_weight, box_orbitals, box_basis, supernode_basis):
    order = ring_order(n_row)
    half_ring = n_row // 2
    to_right = [(order[i], order[(i + 1) % n_row]) for i in range(n_row)]
    to_left = [(order[(i + 1) % n_row], order[i]) for i in range(n_row)]
    _, blocks, parts, depth, width = panel.shape
    tile_count, _, order_b, _ = tiles.shape
    boxes, orbitals = box_orbitals.shape
    total = boxes * orbitals
    rows_chip = BR_DEV * order_b
    slots = 2 * total // n_row
    arrive = (1 + 2 * half_ring) * slots
    half = order_b // 2
    shard_rows = blocks * parts * depth
    lines = -(-2 * total // (16 * LANES)) * 16
    acc_shape = (BR_DEV, order_b, 2 * width)
    acc_out = jax.ShapeDtypeStruct(acc_shape, F32)
    in_vmem = pl.BlockSpec(memory_space=pltpu.VMEM)
    in_smem = pl.BlockSpec(memory_space=pltpu.SMEM)
    params = pltpu.CompilerParams(vmem_limit_bytes=VMEM_LIMIT)
    cost = pl.CostEstimate(flops=2 ** 20, bytes_accessed=2 ** 20, transcendentals=0)

    def call(body, in_specs, out_shape, before, shards, aliases={}):
        weights = pltpu.VMEM((blocks, shards * 2 * LANES, 2 * width), BF16)
        return pl.pallas_call(
            functools.partial(body, n=n_row, depth=depth),
            in_specs=in_specs,
            out_specs=jax.tree.map(lambda _: in_vmem, out_shape),
            out_shape=out_shape,
            scratch_shapes=[*before, weights],
            input_output_aliases=aliases,
            compiler_params=params,
            cost_estimate=cost,
        )

    own = panel.reshape(shard_rows, width)
    own_lines = pl.pallas_call(
        digits_kernel,
        out_shape=jax.ShapeDtypeStruct((lines, width), BF16),
        compiler_params=params,
        cost_estimate=pl.CostEstimate(flops=2 ** 34, bytes_accessed=2 ** 10, transcendentals=0),
    )(box_orbitals)
    pack = pl.pallas_call(
        pack_kernel,
        out_shape=jax.ShapeDtypeStruct((shard_rows + lines, width), BF16),
        compiler_params=params,
        cost_estimate=cost,
    )

    basis_here, wide = pl.pallas_call(
        functools.partial(basis_kernel, n=n_row, rows_chip=rows_chip, slots=slots),
        out_shape=[
            jax.ShapeDtypeStruct((boxes, arrive, box_basis.shape[2]), BF16),
            jax.ShapeDtypeStruct(supernode_basis.shape, F32),
        ],
        compiler_params=params,
        cost_estimate=cost,
    )(box_orbitals, box_basis, supernode_basis)

    left, right = own, own
    seen, hops = [own_lines], [0]
    acc = None
    for h in range(1, half_ring + 1):
        if h < half_ring:
            next_left = lax.ppermute(left, "row", to_right)
            next_right = lax.ppermute(right, "row", to_left)
        else:
            cut = shard_rows // 2
            next_left = lax.ppermute(left[:cut], "row", to_right)
            next_right = lax.ppermute(right[cut:], "row", to_left)
        if h == 1:
            seen += [
                lax.ppermute(own_lines, "row", to_right), lax.ppermute(own_lines, "row", to_left)
            ]
            hops += [-1, 1]
            left, right = pack(next_left, seen[1]), pack(next_right, seen[2])
            continue
        if h == 2:
            acc = call(hop_early, [in_smem] * 2 + [in_vmem] * 4, acc_out, [], 3)(
                tile_slot, tile_col, own, left, right, tiles
            )
        elif h > 2:
            acc = call(
                functools.partial(hop_middle, hop=h - 1),
                [in_smem] * 2 + [in_vmem] * 4,
                acc_out,
                [],
                2,
                aliases={5: 0},
            )(tile_slot, tile_col, left, right, tiles, acc)
        if h == half_ring - 1:
            next_left, basis_here, wide = lax.optimization_barrier((next_left, basis_here, wide))
        left, done = lax.optimization_barrier((next_left, acc))
        right, _ = lax.optimization_barrier((next_right, acc))
        acc = done
        if h < half_ring:
            seen += [left, right]
            hops += [-h, h]
        else:
            seen.append(right)
            hops.append(h)

    swap = [(0, 1), (1, 0)]
    wanted = pl.pallas_call(
        functools.partial(lines_kernel, n=n_row, hops=hops, lines=lines),
        out_shape=jax.ShapeDtypeStruct((n_row * lines, width), BF16),
        compiler_params=params,
        cost_estimate=cost,
    )(*seen)
    left, wanted = lax.optimization_barrier((left, wanted))
    wanted_other = lax.ppermute(wanted, "col", swap)

    half_shape = (BR_DEV, 2, half, width)
    acc, dens = call(
        hop_last,
        [in_smem] * 3 + [in_vmem] * 4,
        [acc_out, jax.ShapeDtypeStruct((BR_DEV, order_b, width), F32)],
        [],
        1,
        aliases={6: 0},
    )(tile_slot, tile_col, pole_weight, left, right, tiles, acc)
    dens, wanted_other = lax.optimization_barrier((dens, wanted_other))
    dens_other = lax.ppermute(dens, "col", swap)
    pick = pl.pallas_call(
        functools.partial(
            pick_kernel, n=n_row, lines=lines, total=total, rows_chip=rows_chip, slots=slots
        ),
        out_shape=jax.ShapeDtypeStruct((arrive, rows_chip), BF16),
        compiler_params=params,
        cost_estimate=pl.CostEstimate(flops=2 ** 32, bytes_accessed=2 ** 20, transcendentals=0),
    )(wanted, wanted_other)
    message = jax.ShapeDtypeStruct((2 * slots, width), BF16)
    kept, *sent = pl.pallas_call(
        select_kernel,
        out_shape=[jax.ShapeDtypeStruct((slots, width), BF16)] + [message] * half_ring,
        compiler_params=params,
        cost_estimate=cost,
    )(pick, dens, dens_other)

    far, near = peers(n_row)
    fetched = []
    for step in range(half_ring):
        pairs = [(2 * r + 1, 2 * (r ^ near[step]) + 1) for r in range(n_row)]
        if step < len(far):
            pairs += [(2 * r, 2 * (r ^ far[step])) for r in range(n_row)]
        fetched.append(lax.ppermute(sent[step], ("row", "col"), pairs))

    turned = pl.pallas_call(
        turn_kernel,
        out_shape=jax.ShapeDtypeStruct((half_ring * slots, width), BF16),
        compiler_params=params,
        cost_estimate=cost,
    )(*fetched)
    passed = lax.ppermute(turned, "col", swap)

    mine, other = pl.pallas_call(
        halves_kernel,
        out_shape=[jax.ShapeDtypeStruct(half_shape, F32)] * 2,
        compiler_params=params,
        cost_estimate=cost,
    )(acc)
    inverse_other = lax.ppermute(other, "col", swap)
    inverse = pl.pallas_call(
        add_kernel,
        out_shape=jax.ShapeDtypeStruct(half_shape, F32),
        compiler_params=params,
        cost_estimate=cost,
    )(mine, inverse_other)
    kept, inverse = lax.optimization_barrier((kept, inverse))
    density = pl.pallas_call(
        density_kernel,
        out_shape=jax.ShapeDtypeStruct((boxes, box_basis.shape[2]), F32),
        compiler_params=params,
    )(kept, *fetched, passed, basis_here, wide)
    return inverse, density


def solution(mesh):
    return jax.shard_map(
        functools.partial(local, mesh.shape["row"]),
        mesh=mesh,
        in_specs=(
            P(("pole", "col"), None, None, "row", None),
            P(("pole", "row", "col"), None, None, None),
            P(("pole", "row", "col")),
            P(("pole", "row", "col")),
            P("pole"),
            P(("pole", "row", "col"), None),
            P(("pole", "row", "col"), None, None),
            P(("pole", "row", "col"), None, None),
        ),
        out_specs=(P(("pole", "row"), None, "col", None), P(("pole", "row", "col"), None)),
        check_vma=False,
    )
```

```python
import functools

import jax
import jax.numpy as jnp
from jax import lax
from jax.experimental import pallas as pl
from jax.experimental.pallas import tpu as pltpu
from jax.sharding import PartitionSpec as P

BR_DEV = 2
LANES = 128
F32 = jnp.float32
BF16 = jnp.bfloat16
VMEM_LIMIT = 8 * 1024 * 1024


def ring_order(n):
    if n <= 8 and n % 2 == 0:
        return list(range(0, n, 2)) + list(range(n - 1, 0, -2))
    return list(range(n))


def shard_row(n, hop):
    row = lax.axis_index("row")
    if ring_order(n) == list(range(n)):
        return lax.rem(row + hop + n, n)
    at = jnp.where(row % 2 == 0, row // 2, n - 1 - row // 2)
    at = lax.rem(at + hop + n, n)
    return jnp.where(at < n // 2, 2 * at, 2 * (n - 1 - at) + 1)


def digits(rows):
    boxes, orbitals = rows.shape
    pieces = [rows[n:n + 1, c:c + LANES] for n in range(boxes) for c in range(0, orbitals, LANES)]
    lines = [piece // 256 for piece in pieces] + [piece % 256 for piece in pieces]
    pad = -len(lines) % 16
    lines.append(jnp.zeros((pad, LANES), jnp.int32))
    return jnp.concatenate(lines, axis=0).astype(F32).astype(BF16)


def undigits(lines, total):
    count = total // LANES
    lines = lines.astype(F32)
    whole = lines[:count] * 256.0 + lines[count:2 * count]
    return jnp.concatenate([whole[i:i + 1] for i in range(count)], axis=1)


def digits_kernel(wanted, out):
    out[...] = digits(wanted[...])


def pack_kernel(rows, lines, out):
    out[:rows.shape[0], :] = rows[...]
    out[rows.shape[0]:, :] = lines[...]


def place(part, block, depth, first):
    reps = LANES // depth
    row = lax.broadcasted_iota(jnp.int32, (LANES, part.shape[1]), 0)
    inside = (row // depth) == first
    spread = []
    for p in range(2):
        rows = part[(2 * block + p) * depth:(2 * block + p + 1) * depth, :].astype(F32)
        spread.append(jnp.where(inside, jnp.concatenate([rows] * reps, axis=0), 0.0))
    upper = jnp.concatenate([spread[0], spread[1]], axis=1)
    lower = jnp.concatenate([-spread[1], spread[0]], axis=1)
    return jnp.concatenate([upper, lower], axis=0).astype(BF16)


def accumulate(slots, cols, tiles, shards, acc, weights):
    blocks = weights.shape[0]
    starts = []
    for s, (row, depth, parts) in enumerate(shards):
        reps = LANES // depth
        starts.append(pl.multiple_of(row // reps * LANES, LANES))
        share = blocks // len(parts)
        for b in range(blocks):
            weights[b, s * 2 * LANES:(s + 1) * 2 * LANES, :] = place(
                parts[b // share], b % share, depth, row % reps
            )
    for t in range(tiles.shape[0]):
        left = jnp.concatenate(
            [tiles[t, p, :, pl.ds(start, LANES)] for start in starts for p in range(2)], axis=1
        )
        acc[slots[t]] += jnp.dot(left, weights[cols[t]], preferred_element_type=F32)


def hop_early(slots, cols, own, from_left, from_right, tiles, out, weights, *, n, depth):
    out[...] = jnp.zeros_like(out)
    shards = [
        (shard_row(n, 0), depth, [own]),
        (shard_row(n, -1), depth, [from_left]),
        (shard_row(n, 1), depth, [from_right]),
    ]
    accumulate(slots, cols, tiles, shards, out, weights)


def hop_middle(slots, cols, from_left, from_right, tiles, start, out, weights, *, n, depth, hop):
    del start
    shards = [
        (shard_row(n, -hop), depth, [from_left]), (shard_row(n, hop), depth, [from_right])
    ]
    accumulate(slots, cols, tiles, shards, out, weights)


def hop_last(slots, cols, pole_weight, low, high, tiles, start, out, dens, weights, *, n, depth):
    del start
    accumulate(slots, cols, tiles, [(shard_row(n, n // 2), depth, [low, high])], out, weights)
    width = dens.shape[2]
    for slot in range(out.shape[0]):
        dens[slot] = -(pole_weight[0] * out[slot, :, width:] + pole_weight[1] * out[slot, :, :width])


def halves_kernel(acc, mine, other):
    col = lax.axis_index("col")
    half = mine.shape[2]
    width = mine.shape[3]
    for slot in range(acc.shape[0]):
        for p in range(2):
            cut = slice(p * width, (p + 1) * width)
            mine[slot, p] = -acc[slot, pl.ds(pl.multiple_of(col * half, half), half), cut]
            other[slot, p] = -acc[slot, pl.ds(pl.multiple_of((1 - col) * half, half), half), cut]


def earlier(total):
    first = lax.broadcasted_iota(jnp.int32, (total, total), 0)
    second = lax.broadcasted_iota(jnp.int32, (total, total), 1)
    return (first < second).astype(F32).astype(BF16)


def peers(n):
    half = n // 2
    return list(range(n - 1, half + 1, -1)) + [half], list(range(1, half)) + [half + 1]


def place_of(chip, n):
    apart = chip ^ lax.axis_index("row")
    place = jnp.zeros_like(apart)
    for core, steps in enumerate(peers(n)):
        first = jnp.where(lax.axis_index("col") == core, 1, 1 + n // 2)
        for step, k in enumerate(steps):
            place = jnp.where(apart == k, first + step, place)
    return place


def basis_kernel(wanted, basis, supernode, out, wide, *, n, rows_chip, slots):
    wide[...] = supernode[...].astype(F32)
    boxes, orbitals, _ = basis.shape
    total = boxes * orbitals
    rows = wanted[...]
    asked = jnp.concatenate([rows[b:b + 1] for b in range(boxes)], axis=1)
    source = asked // rows_chip
    marks = (lax.broadcasted_iota(jnp.int32, (n, total), 0) == source).astype(F32)
    counts = jnp.dot(marks.astype(BF16), earlier(total), preferred_element_type=F32)
    rank = jnp.sum(marks * counts, axis=0, keepdims=True).astype(jnp.int32)
    slot = place_of(source, n) * slots + rank
    index = lax.broadcasted_iota(jnp.int32, (out.shape[1], orbitals), 0)
    for b in range(boxes):
        pick = (index == slot[:, b * orbitals:(b + 1) * orbitals]).astype(F32).astype(BF16)
        out[b] = jnp.dot(pick, basis[b], preferred_element_type=F32).astype(BF16)


def lines_kernel(*refs, n, hops, lines):
    *shards, out = refs
    for ref, hop in zip(shards, hops):
        at = pl.multiple_of(shard_row(n, hop) * lines, lines)
        out[pl.ds(at, lines), :] = ref[ref.shape[0] - lines:, :]


def pick_kernel(mine, theirs, out, *, n, lines, total, rows_chip, slots):
    row = lax.axis_index("row")
    col = lax.axis_index("col")
    far, near = peers(n)
    far = far + near[-1:]

    def asked_by(chip, own):
        at = pl.ds(pl.multiple_of(chip * lines, lines), lines)
        return undigits(jnp.where(own, mine[at, :].astype(F32), theirs[at, :].astype(F32)), total)

    asked = [asked_by(row, True)]
    for step in range(n // 2):
        chip = row ^ jnp.where(col == 0, far[step], near[step])
        asked += [asked_by(chip, col == 0), asked_by(chip, col == 1)]
    count = len(asked)
    asked = jnp.concatenate(asked, axis=0).astype(jnp.int32)
    here = (asked // rows_chip) == row
    local = (asked % rows_chip).astype(F32)
    rank = jnp.dot(
        here.astype(F32).astype(BF16), earlier(total), preferred_element_type=F32
    ).astype(jnp.int32)
    rank = jnp.where(here, rank, -1)
    index = lax.broadcasted_iota(jnp.int32, (slots, total), 0)
    lane = lax.broadcasted_iota(jnp.int32, (slots, rows_chip), 1)
    for d in range(count):
        chosen = jnp.where(index == rank[d:d + 1], local[d:d + 1], 0.0)
        at = jnp.sum(chosen, axis=1, keepdims=True).astype(jnp.int32)
        out[d * slots:(d + 1) * slots, :] = (lane == at).astype(F32).astype(BF16)


def add_kernel(mine, theirs, out):
    out[...] = mine[...] + theirs[...]


def select_kernel(pick, mine, theirs, *outs):
    rows = pick.shape[1]
    total = (mine[...] + theirs[...]).reshape(rows, mine.shape[2]).astype(BF16)
    rows_out = jnp.dot(pick[...], total, preferred_element_type=F32).astype(BF16)
    at = 0
    for out in outs:
        out[...] = rows_out[at:at + out.shape[0]]
        at += out.shape[0]


def turn_kernel(*refs):
    *parts, out = refs
    slots = out.shape[0] // len(parts)
    at = pl.ds(pl.multiple_of((1 - lax.axis_index("col")) * slots, slots), slots)
    for i, part in enumerate(parts):
        out[i * slots:(i + 1) * slots] = part[at, :]


def first_kernel(*refs):
    own, *parts, basis, out = refs
    slots = own.shape[0]
    at = pl.ds(pl.multiple_of(lax.axis_index("col") * slots, slots), slots)
    arrived = jnp.concatenate([own[...]] + [part[at, :] for part in parts], axis=0)
    for n in range(basis.shape[0]):
        out[n] = lax.dot_general(
            arrived,
            basis[n, :arrived.shape[0], :],
            (((0,), (0,)), ((), ())),
            preferred_element_type=F32,
        )


def density_kernel(passed, first, basis, supernode, out):
    for n in range(basis.shape[0]):
        projected = first[n] + lax.dot_general(
            passed[...],
            basis[n, basis.shape[1] - passed.shape[0]:, :],
            (((0,), (0,)), ((), ())),
            preferred_element_type=F32,
        )
        out[n:n + 1, :] = jnp.sum(supernode[n] * projected, axis=0, keepdims=True)


def local(n_row, panel, tiles, tile_slot, tile_col, pole_weight, box_orbitals, box_basis, supernode_basis):
    order = ring_order(n_row)
    half_ring = n_row // 2
    to_right = [(order[i], order[(i + 1) % n_row]) for i in range(n_row)]
    to_left = [(order[(i + 1) % n_row], order[i]) for i in range(n_row)]
    _, blocks, parts, depth, width = panel.shape
    tile_count, _, order_b, _ = tiles.shape
    boxes, orbitals = box_orbitals.shape
    total = boxes * orbitals
    rows_chip = BR_DEV * order_b
    slots = 2 * total // n_row
    arrive = (1 + 2 * half_ring) * slots
    half = order_b // 2
    shard_rows = blocks * parts * depth
    lines = -(-2 * total // (16 * LANES)) * 16
    acc_shape = (BR_DEV, order_b, 2 * width)
    acc_out = jax.ShapeDtypeStruct(acc_shape, F32)
    in_vmem = pl.BlockSpec(memory_space=pltpu.VMEM)
    in_smem = pl.BlockSpec(memory_space=pltpu.SMEM)
    params = pltpu.CompilerParams(vmem_limit_bytes=VMEM_LIMIT)
    cost = pl.CostEstimate(flops=2 ** 20, bytes_accessed=2 ** 20, transcendentals=0)

    def call(body, in_specs, out_shape, before, shards, aliases={}):
        weights = pltpu.VMEM((blocks, shards * 2 * LANES, 2 * width), BF16)
        return pl.pallas_call(
            functools.partial(body, n=n_row, depth=depth),
            in_specs=in_specs,
            out_specs=jax.tree.map(lambda _: in_vmem, out_shape),
            out_shape=out_shape,
            scratch_shapes=[*before, weights],
            input_output_aliases=aliases,
            compiler_params=params,
            cost_estimate=cost,
        )

    own = panel.reshape(shard_rows, width)
    own_lines = pl.pallas_call(
        digits_kernel,
        out_shape=jax.ShapeDtypeStruct((lines, width), BF16),
        compiler_params=params,
        cost_estimate=pl.CostEstimate(flops=2 ** 34, bytes_accessed=2 ** 10, transcendentals=0),
    )(box_orbitals)
    pack = pl.pallas_call(
        pack_kernel,
        out_shape=jax.ShapeDtypeStruct((shard_rows + lines, width), BF16),
        compiler_params=params,
        cost_estimate=cost,
    )

    basis_here, wide = pl.pallas_call(
        functools.partial(basis_kernel, n=n_row, rows_chip=rows_chip, slots=slots),
        out_shape=[
            jax.ShapeDtypeStruct((boxes, arrive, box_basis.shape[2]), BF16),
            jax.ShapeDtypeStruct(supernode_basis.shape, F32),
        ],
        compiler_params=params,
        cost_estimate=cost,
    )(box_orbitals, box_basis, supernode_basis)

    left, right = own, own
    seen, hops = [own_lines], [0]
    acc = None
    for h in range(1, half_ring + 1):
        if h < half_ring:
            next_left = lax.ppermute(left, "row", to_right)
            next_right = lax.ppermute(right, "row", to_left)
        else:
            cut = shard_rows // 2
            next_left = lax.ppermute(left[:cut], "row", to_right)
            next_right = lax.ppermute(right[cut:], "row", to_left)
        if h == 1:
            seen += [
                lax.ppermute(own_lines, "row", to_right), lax.ppermute(own_lines, "row", to_left)
            ]
            hops += [-1, 1]
            left, right = pack(next_left, seen[1]), pack(next_right, seen[2])
            continue
        if h == 2:
            acc = call(hop_early, [in_smem] * 2 + [in_vmem] * 4, acc_out, [], 3)(
                tile_slot, tile_col, own, left, right, tiles
            )
        elif h > 2:
            acc = call(
                functools.partial(hop_middle, hop=h - 1),
                [in_smem] * 2 + [in_vmem] * 4,
                acc_out,
                [],
                2,
                aliases={5: 0},
            )(tile_slot, tile_col, left, right, tiles, acc)
        if h == half_ring - 1:
            next_left, basis_here, wide = lax.optimization_barrier((next_left, basis_here, wide))
        left, done = lax.optimization_barrier((next_left, acc))
        right, _ = lax.optimization_barrier((next_right, acc))
        acc = done
        if h < half_ring:
            seen += [left, right]
            hops += [-h, h]
        else:
            seen.append(right)
            hops.append(h)

    swap = [(0, 1), (1, 0)]
    wanted = pl.pallas_call(
        functools.partial(lines_kernel, n=n_row, hops=hops, lines=lines),
        out_shape=jax.ShapeDtypeStruct((n_row * lines, width), BF16),
        compiler_params=params,
        cost_estimate=cost,
    )(*seen)
    left, wanted = lax.optimization_barrier((left, wanted))
    wanted_other = lax.ppermute(wanted, "col", swap)

    half_shape = (BR_DEV, 2, half, width)
    acc, dens = call(
        hop_last,
        [in_smem] * 3 + [in_vmem] * 4,
        [acc_out, jax.ShapeDtypeStruct((BR_DEV, order_b, width), F32)],
        [],
        1,
        aliases={6: 0},
    )(tile_slot, tile_col, pole_weight, left, right, tiles, acc)
    dens, wanted_other = lax.optimization_barrier((dens, wanted_other))
    dens_other = lax.ppermute(dens, "col", swap)
    pick = pl.pallas_call(
        functools.partial(
            pick_kernel, n=n_row, lines=lines, total=total, rows_chip=rows_chip, slots=slots
        ),
        out_shape=jax.ShapeDtypeStruct((arrive, rows_chip), BF16),
        compiler_params=params,
        cost_estimate=pl.CostEstimate(flops=2 ** 32, bytes_accessed=2 ** 20, transcendentals=0),
    )(wanted, wanted_other)
    message = jax.ShapeDtypeStruct((2 * slots, width), BF16)
    kept, *sent = pl.pallas_call(
        select_kernel,
        out_shape=[jax.ShapeDtypeStruct((slots, width), BF16)] + [message] * half_ring,
        compiler_params=params,
        cost_estimate=cost,
    )(pick, dens, dens_other)

    far, near = peers(n_row)
    fetched = []
    for step in range(half_ring):
        pairs = [(2 * r + 1, 2 * (r ^ near[step]) + 1) for r in range(n_row)]
        if step < len(far):
            pairs += [(2 * r, 2 * (r ^ far[step])) for r in range(n_row)]
        fetched.append(lax.ppermute(sent[step], ("row", "col"), pairs))

    mine, other = pl.pallas_call(
        halves_kernel,
        out_shape=[jax.ShapeDtypeStruct(half_shape, F32)] * 2,
        compiler_params=params,
        cost_estimate=cost,
    )(acc)
    inverse_other = lax.ppermute(other, "col", swap)
    inverse = pl.pallas_call(
        add_kernel,
        out_shape=jax.ShapeDtypeStruct(half_shape, F32),
        compiler_params=params,
        cost_estimate=cost,
    )(mine, inverse_other)
    fetched[0], inverse = lax.optimization_barrier((fetched[0], inverse))
    turned = pl.pallas_call(
        turn_kernel,
        out_shape=jax.ShapeDtypeStruct((half_ring * slots, width), BF16),
        compiler_params=params,
        cost_estimate=cost,
    )(*fetched)
    passed = lax.ppermute(turned, "col", swap)
    first = pl.pallas_call(
        first_kernel,
        out_shape=jax.ShapeDtypeStruct((boxes, width, box_basis.shape[2]), F32),
        compiler_params=params,
        cost_estimate=cost,
    )(kept, *fetched, basis_here)
    density = pl.pallas_call(
        density_kernel,
        out_shape=jax.ShapeDtypeStruct((boxes, box_basis.shape[2]), F32),
        compiler_params=params,
    )(passed, first, basis_here, wide)
    return inverse, density


def solution(mesh):
    return jax.shard_map(
        functools.partial(local, mesh.shape["row"]),
        mesh=mesh,
        in_specs=(
            P(("pole", "col"), None, None, "row", None),
            P(("pole", "row", "col"), None, None, None),
            P(("pole", "row", "col")),
            P(("pole", "row", "col")),
            P("pole"),
            P(("pole", "row", "col"), None),
            P(("pole", "row", "col"), None, None),
            P(("pole", "row", "col"), None, None),
        ),
        out_specs=(P(("pole", "row"), None, "col", None), P(("pole", "row", "col"), None)),
        check_vma=False,
    )
```

```python
import functools

import jax
import jax.numpy as jnp
from jax import lax
from jax.experimental import pallas as pl
from jax.experimental.pallas import tpu as pltpu
from jax.sharding import PartitionSpec as P

BR_DEV = 2
LANES = 128
F32 = jnp.float32
BF16 = jnp.bfloat16
VMEM_LIMIT = 8 * 1024 * 1024


def ring_order(n):
    if n <= 8 and n % 2 == 0:
        return list(range(0, n, 2)) + list(range(n - 1, 0, -2))
    return list(range(n))


def shard_row(n, hop):
    row = lax.axis_index("row")
    if ring_order(n) == list(range(n)):
        return lax.rem(row + hop + n, n)
    at = jnp.where(row % 2 == 0, row // 2, n - 1 - row // 2)
    at = lax.rem(at + hop + n, n)
    return jnp.where(at < n // 2, 2 * at, 2 * (n - 1 - at) + 1)


def digits(rows):
    boxes, orbitals = rows.shape
    pieces = [rows[n:n + 1, c:c + LANES] for n in range(boxes) for c in range(0, orbitals, LANES)]
    lines = [piece // 256 for piece in pieces] + [piece % 256 for piece in pieces]
    pad = -len(lines) % 16
    lines.append(jnp.zeros((pad, LANES), jnp.int32))
    return jnp.concatenate(lines, axis=0).astype(F32).astype(BF16)


def undigits(lines, total):
    count = total // LANES
    lines = lines.astype(F32)
    whole = lines[:count] * 256.0 + lines[count:2 * count]
    return jnp.concatenate([whole[i:i + 1] for i in range(count)], axis=1)


def digits_kernel(wanted, out):
    out[...] = digits(wanted[...])


def pack_kernel(rows, lines, out):
    out[:rows.shape[0], :] = rows[...]
    out[rows.shape[0]:, :] = lines[...]


def place(part, block, depth, first):
    reps = LANES // depth
    row = lax.broadcasted_iota(jnp.int32, (LANES, part.shape[1]), 0)
    inside = (row // depth) == first
    spread = []
    for p in range(2):
        rows = part[(2 * block + p) * depth:(2 * block + p + 1) * depth, :].astype(F32)
        spread.append(jnp.where(inside, jnp.concatenate([rows] * reps, axis=0), 0.0))
    upper = jnp.concatenate([spread[0], spread[1]], axis=1)
    lower = jnp.concatenate([-spread[1], spread[0]], axis=1)
    return jnp.concatenate([upper, lower], axis=0).astype(BF16)


def accumulate(slots, cols, tiles, shards, acc, weights):
    blocks = weights.shape[0]
    starts = []
    for s, (row, depth, parts) in enumerate(shards):
        reps = LANES // depth
        starts.append(pl.multiple_of(row // reps * LANES, LANES))
        share = blocks // len(parts)
        for b in range(blocks):
            weights[b, s * 2 * LANES:(s + 1) * 2 * LANES, :] = place(
                parts[b // share], b % share, depth, row % reps
            )
    for t in range(tiles.shape[0]):
        left = jnp.concatenate(
            [tiles[t, p, :, pl.ds(start, LANES)] for start in starts for p in range(2)], axis=1
        )
        acc[slots[t]] += jnp.dot(left, weights[cols[t]], preferred_element_type=F32)


def hop_early(slots, cols, own, from_left, from_right, tiles, out, weights, *, n, depth):
    out[...] = jnp.zeros_like(out)
    shards = [
        (shard_row(n, 0), depth, [own]),
        (shard_row(n, -1), depth, [from_left]),
        (shard_row(n, 1), depth, [from_right]),
    ]
    accumulate(slots, cols, tiles, shards, out, weights)


def hop_middle(slots, cols, from_left, from_right, tiles, start, out, weights, *, n, depth, hop):
    del start
    shards = [
        (shard_row(n, -hop), depth, [from_left]), (shard_row(n, hop), depth, [from_right])
    ]
    accumulate(slots, cols, tiles, shards, out, weights)


def hop_last(slots, cols, pole_weight, low, high, tiles, start, out, dens, weights, *, n, depth):
    del start
    accumulate(slots, cols, tiles, [(shard_row(n, n // 2), depth, [low, high])], out, weights)
    width = dens.shape[2]
    for slot in range(out.shape[0]):
        dens[slot] = -(pole_weight[0] * out[slot, :, width:] + pole_weight[1] * out[slot, :, :width])


def halves_kernel(acc, mine, other):
    col = lax.axis_index("col")
    half = mine.shape[2]
    width = mine.shape[3]
    for slot in range(acc.shape[0]):
        for p in range(2):
            cut = slice(p * width, (p + 1) * width)
            mine[slot, p] = -acc[slot, pl.ds(pl.multiple_of(col * half, half), half), cut]
            other[slot, p] = -acc[slot, pl.ds(pl.multiple_of((1 - col) * half, half), half), cut]


def earlier(total):
    first = lax.broadcasted_iota(jnp.int32, (total, total), 0)
    second = lax.broadcasted_iota(jnp.int32, (total, total), 1)
    return (first < second).astype(F32).astype(BF16)


def peers(n):
    half = n // 2
    return list(range(n - 1, half + 1, -1)) + [half], list(range(1, half)) + [half + 1]


def place_of(chip, n):
    apart = chip ^ lax.axis_index("row")
    place = jnp.zeros_like(apart)
    for core, steps in enumerate(peers(n)):
        first = jnp.where(lax.axis_index("col") == core, 1, 1 + n // 2)
        for step, k in enumerate(steps):
            place = jnp.where(apart == k, first + step, place)
    return place


def basis_kernel(wanted, basis, supernode, out, wide, *, n, rows_chip, slots):
    wide[...] = supernode[...].astype(F32)
    boxes, orbitals, _ = basis.shape
    total = boxes * orbitals
    rows = wanted[...]
    asked = jnp.concatenate([rows[b:b + 1] for b in range(boxes)], axis=1)
    source = asked // rows_chip
    marks = (lax.broadcasted_iota(jnp.int32, (n, total), 0) == source).astype(F32)
    counts = jnp.dot(marks.astype(BF16), earlier(total), preferred_element_type=F32)
    rank = jnp.sum(marks * counts, axis=0, keepdims=True).astype(jnp.int32)
    slot = place_of(source, n) * slots + rank
    index = lax.broadcasted_iota(jnp.int32, (out.shape[1], orbitals), 0)
    for b in range(boxes):
        pick = (index == slot[:, b * orbitals:(b + 1) * orbitals]).astype(F32).astype(BF16)
        out[b] = jnp.dot(pick, basis[b], preferred_element_type=F32).astype(BF16)


def lines_kernel(*refs, n, hops, lines):
    *shards, out = refs
    for ref, hop in zip(shards, hops):
        at = pl.multiple_of(shard_row(n, hop) * lines, lines)
        out[pl.ds(at, lines), :] = ref[ref.shape[0] - lines:, :]


def pick_kernel(mine, theirs, out, *, n, lines, total, rows_chip, slots):
    row = lax.axis_index("row")
    col = lax.axis_index("col")
    far, near = peers(n)
    far = far + near[-1:]

    def asked_by(chip, own):
        at = pl.ds(pl.multiple_of(chip * lines, lines), lines)
        return undigits(jnp.where(own, mine[at, :].astype(F32), theirs[at, :].astype(F32)), total)

    asked = [asked_by(row, True)]
    for step in range(n // 2):
        chip = row ^ jnp.where(col == 0, far[step], near[step])
        asked += [asked_by(chip, col == 0), asked_by(chip, col == 1)]
    count = len(asked)
    asked = jnp.concatenate(asked, axis=0).astype(jnp.int32)
    here = (asked // rows_chip) == row
    local = (asked % rows_chip).astype(F32)
    rank = jnp.dot(
        here.astype(F32).astype(BF16), earlier(total), preferred_element_type=F32
    ).astype(jnp.int32)
    rank = jnp.where(here, rank, -1)
    index = lax.broadcasted_iota(jnp.int32, (slots, total), 0)
    lane = lax.broadcasted_iota(jnp.int32, (slots, rows_chip), 1)
    for d in range(count):
        chosen = jnp.where(index == rank[d:d + 1], local[d:d + 1], 0.0)
        at = jnp.sum(chosen, axis=1, keepdims=True).astype(jnp.int32)
        out[d * slots:(d + 1) * slots, :] = (lane == at).astype(F32).astype(BF16)


def add_kernel(mine, theirs, out):
    out[...] = mine[...] + theirs[...]


def select_kernel(pick, mine, theirs, *outs):
    rows = pick.shape[1]
    total = (mine[...] + theirs[...]).reshape(rows, mine.shape[2]).astype(BF16)
    rows_out = jnp.dot(pick[...], total, preferred_element_type=F32).astype(BF16)
    at = 0
    for out in outs:
        out[...] = rows_out[at:at + out.shape[0]]
        at += out.shape[0]


def turn_kernel(*refs):
    *parts, out = refs
    slots = out.shape[0] // len(parts)
    at = pl.ds(pl.multiple_of((1 - lax.axis_index("col")) * slots, slots), slots)
    for i, part in enumerate(parts):
        out[i * slots:(i + 1) * slots] = part[at, :]


def first_kernel(*refs):
    own, *parts, basis, out = refs
    slots = own.shape[0]
    at = pl.ds(pl.multiple_of(lax.axis_index("col") * slots, slots), slots)
    arrived = jnp.concatenate([own[...]] + [part[at, :] for part in parts], axis=0)
    for n in range(basis.shape[0]):
        out[n] = lax.dot_general(
            arrived,
            basis[n, :arrived.shape[0], :],
            (((0,), (0,)), ((), ())),
            preferred_element_type=F32,
        )


def density_kernel(passed, first, basis, supernode, out):
    for n in range(basis.shape[0]):
        projected = first[n] + lax.dot_general(
            passed[...],
            basis[n, basis.shape[1] - passed.shape[0]:, :],
            (((0,), (0,)), ((), ())),
            preferred_element_type=F32,
        )
        out[n:n + 1, :] = jnp.sum(supernode[n] * projected, axis=0, keepdims=True)


def local(n_row, panel, tiles, tile_slot, tile_col, pole_weight, box_orbitals, box_basis, supernode_basis):
    order = ring_order(n_row)
    half_ring = n_row // 2
    to_right = [(order[i], order[(i + 1) % n_row]) for i in range(n_row)]
    to_left = [(order[(i + 1) % n_row], order[i]) for i in range(n_row)]
    _, blocks, parts, depth, width = panel.shape
    tile_count, _, order_b, _ = tiles.shape
    boxes, orbitals = box_orbitals.shape
    total = boxes * orbitals
    rows_chip = BR_DEV * order_b
    slots = 2 * total // n_row
    arrive = (1 + 2 * half_ring) * slots
    half = order_b // 2
    shard_rows = blocks * parts * depth
    lines = -(-2 * total // (16 * LANES)) * 16
    acc_shape = (BR_DEV, order_b, 2 * width)
    acc_out = jax.ShapeDtypeStruct(acc_shape, F32)
    in_vmem = pl.BlockSpec(memory_space=pltpu.VMEM)
    in_smem = pl.BlockSpec(memory_space=pltpu.SMEM)
    params = pltpu.CompilerParams(vmem_limit_bytes=VMEM_LIMIT)
    cost = pl.CostEstimate(flops=2 ** 20, bytes_accessed=2 ** 20, transcendentals=0)

    def call(body, in_specs, out_shape, before, shards, aliases={}):
        weights = pltpu.VMEM((blocks, shards * 2 * LANES, 2 * width), BF16)
        return pl.pallas_call(
            functools.partial(body, n=n_row, depth=depth),
            in_specs=in_specs,
            out_specs=jax.tree.map(lambda _: in_vmem, out_shape),
            out_shape=out_shape,
            scratch_shapes=[*before, weights],
            input_output_aliases=aliases,
            compiler_params=params,
            cost_estimate=cost,
        )

    own = panel.reshape(shard_rows, width)
    own_lines = pl.pallas_call(
        digits_kernel,
        out_shape=jax.ShapeDtypeStruct((lines, width), BF16),
        compiler_params=params,
        cost_estimate=pl.CostEstimate(flops=2 ** 34, bytes_accessed=2 ** 10, transcendentals=0),
    )(box_orbitals)
    pack = pl.pallas_call(
        pack_kernel,
        out_shape=jax.ShapeDtypeStruct((shard_rows + lines, width), BF16),
        compiler_params=params,
        cost_estimate=cost,
    )

    basis_here, wide = pl.pallas_call(
        functools.partial(basis_kernel, n=n_row, rows_chip=rows_chip, slots=slots),
        out_shape=[
            jax.ShapeDtypeStruct((boxes, arrive, box_basis.shape[2]), BF16),
            jax.ShapeDtypeStruct(supernode_basis.shape, F32),
        ],
        compiler_params=params,
        cost_estimate=cost,
    )(box_orbitals, box_basis, supernode_basis)

    left, right = own, own
    seen, hops = [own_lines], [0]
    acc = None
    for h in range(1, half_ring + 1):
        if h < half_ring:
            next_left = lax.ppermute(left, "row", to_right)
            next_right = lax.ppermute(right, "row", to_left)
        else:
            cut = shard_rows // 2
            next_left = lax.ppermute(left[:cut], "row", to_right)
            next_right = lax.ppermute(right[cut:], "row", to_left)
        if h == 1:
            seen += [
                lax.ppermute(own_lines, "row", to_right), lax.ppermute(own_lines, "row", to_left)
            ]
            hops += [-1, 1]
            left, right = pack(next_left, seen[1]), pack(next_right, seen[2])
            continue
        if h == 2:
            acc = call(hop_early, [in_smem] * 2 + [in_vmem] * 4, acc_out, [], 3)(
                tile_slot, tile_col, own, left, right, tiles
            )
        elif h > 2:
            acc = call(
                functools.partial(hop_middle, hop=h - 1),
                [in_smem] * 2 + [in_vmem] * 4,
                acc_out,
                [],
                2,
                aliases={5: 0},
            )(tile_slot, tile_col, left, right, tiles, acc)
        left, done = lax.optimization_barrier((next_left, acc))
        right, _ = lax.optimization_barrier((next_right, acc))
        acc = done
        if h < half_ring:
            seen += [left, right]
            hops += [-h, h]
        else:
            seen.append(right)
            hops.append(h)

    swap = [(0, 1), (1, 0)]
    wanted = pl.pallas_call(
        functools.partial(lines_kernel, n=n_row, hops=hops, lines=lines),
        out_shape=jax.ShapeDtypeStruct((n_row * lines, width), BF16),
        compiler_params=params,
        cost_estimate=cost,
    )(*seen)
    left, wanted, basis_here, wide = lax.optimization_barrier((left, wanted, basis_here, wide))
    wanted_other = lax.ppermute(wanted, "col", swap)

    half_shape = (BR_DEV, 2, half, width)
    acc, dens = call(
        hop_last,
        [in_smem] * 3 + [in_vmem] * 4,
        [acc_out, jax.ShapeDtypeStruct((BR_DEV, order_b, width), F32)],
        [],
        1,
        aliases={6: 0},
    )(tile_slot, tile_col, pole_weight, left, right, tiles, acc)
    dens, wanted_other = lax.optimization_barrier((dens, wanted_other))
    dens_other = lax.ppermute(dens, "col", swap)
    pick = pl.pallas_call(
        functools.partial(
            pick_kernel, n=n_row, lines=lines, total=total, rows_chip=rows_chip, slots=slots
        ),
        out_shape=jax.ShapeDtypeStruct((arrive, rows_chip), BF16),
        compiler_params=params,
        cost_estimate=pl.CostEstimate(flops=2 ** 32, bytes_accessed=2 ** 20, transcendentals=0),
    )(wanted, wanted_other)
    message = jax.ShapeDtypeStruct((2 * slots, width), BF16)
    kept, *sent = pl.pallas_call(
        select_kernel,
        out_shape=[jax.ShapeDtypeStruct((slots, width), BF16)] + [message] * half_ring,
        compiler_params=params,
        cost_estimate=cost,
    )(pick, dens, dens_other)

    far, near = peers(n_row)
    fetched = []
    for step in range(half_ring):
        pairs = [(2 * r + 1, 2 * (r ^ near[step]) + 1) for r in range(n_row)]
        if step < len(far):
            pairs += [(2 * r, 2 * (r ^ far[step])) for r in range(n_row)]
        fetched.append(lax.ppermute(sent[step], ("row", "col"), pairs))

    mine, other = pl.pallas_call(
        halves_kernel,
        out_shape=[jax.ShapeDtypeStruct(half_shape, F32)] * 2,
        compiler_params=params,
        cost_estimate=cost,
    )(acc)
    inverse_other = lax.ppermute(other, "col", swap)
    inverse = pl.pallas_call(
        add_kernel,
        out_shape=jax.ShapeDtypeStruct(half_shape, F32),
        compiler_params=params,
        cost_estimate=cost,
    )(mine, inverse_other)
    fetched[0], inverse = lax.optimization_barrier((fetched[0], inverse))
    turned = pl.pallas_call(
        turn_kernel,
        out_shape=jax.ShapeDtypeStruct((half_ring * slots, width), BF16),
        compiler_params=params,
        cost_estimate=cost,
    )(*fetched)
    passed = lax.ppermute(turned, "col", swap)
    first = pl.pallas_call(
        first_kernel,
        out_shape=jax.ShapeDtypeStruct((boxes, width, box_basis.shape[2]), F32),
        compiler_params=params,
        cost_estimate=cost,
    )(kept, *fetched, basis_here)
    density = pl.pallas_call(
        density_kernel,
        out_shape=jax.ShapeDtypeStruct((boxes, box_basis.shape[2]), F32),
        compiler_params=params,
    )(passed, first, basis_here, wide)
    return inverse, density


def solution(mesh):
    return jax.shard_map(
        functools.partial(local, mesh.shape["row"]),
        mesh=mesh,
        in_specs=(
            P(("pole", "col"), None, None, "row", None),
            P(("pole", "row", "col"), None, None, None),
            P(("pole", "row", "col")),
            P(("pole", "row", "col")),
            P("pole"),
            P(("pole", "row", "col"), None),
            P(("pole", "row", "col"), None, None),
            P(("pole", "row", "col"), None, None),
        ),
        out_specs=(P(("pole", "row"), None, "col", None), P(("pole", "row", "col"), None)),
        check_vma=False,
    )
```

```python
import functools

import jax
import jax.numpy as jnp
from jax import lax
from jax.experimental import pallas as pl
from jax.experimental.pallas import tpu as pltpu
from jax.sharding import PartitionSpec as P

BR_DEV = 2
LANES = 128
F32 = jnp.float32
BF16 = jnp.bfloat16
VMEM_LIMIT = 8 * 1024 * 1024


def ring_order(n):
    if n <= 8 and n % 2 == 0:
        return list(range(0, n, 2)) + list(range(n - 1, 0, -2))
    return list(range(n))


def shard_row(n, hop):
    row = lax.axis_index("row")
    if ring_order(n) == list(range(n)):
        return lax.rem(row + hop + n, n)
    at = jnp.where(row % 2 == 0, row // 2, n - 1 - row // 2)
    at = lax.rem(at + hop + n, n)
    return jnp.where(at < n // 2, 2 * at, 2 * (n - 1 - at) + 1)


def digits(rows):
    boxes, orbitals = rows.shape
    pieces = [rows[n:n + 1, c:c + LANES] for n in range(boxes) for c in range(0, orbitals, LANES)]
    lines = [piece // 256 for piece in pieces] + [piece % 256 for piece in pieces]
    pad = -len(lines) % 16
    lines.append(jnp.zeros((pad, LANES), jnp.int32))
    return jnp.concatenate(lines, axis=0).astype(F32).astype(BF16)


def undigits(lines, total):
    count = total // LANES
    lines = lines.astype(F32)
    whole = lines[:count] * 256.0 + lines[count:2 * count]
    return jnp.concatenate([whole[i:i + 1] for i in range(count)], axis=1)


def digits_kernel(wanted, out):
    out[...] = digits(wanted[...])


def pack_kernel(rows, lines, out):
    out[:rows.shape[0], :] = rows[...]
    out[rows.shape[0]:, :] = lines[...]


def place(part, block, depth, first):
    reps = LANES // depth
    row = lax.broadcasted_iota(jnp.int32, (LANES, part.shape[1]), 0)
    inside = (row // depth) == first
    spread = []
    for p in range(2):
        rows = part[(2 * block + p) * depth:(2 * block + p + 1) * depth, :].astype(F32)
        spread.append(jnp.where(inside, jnp.concatenate([rows] * reps, axis=0), 0.0))
    upper = jnp.concatenate([spread[0], spread[1]], axis=1)
    lower = jnp.concatenate([-spread[1], spread[0]], axis=1)
    return jnp.concatenate([upper, lower], axis=0).astype(BF16)


def accumulate(slots, cols, tiles, shards, acc, weights):
    blocks = weights.shape[0]
    starts = []
    for s, (row, depth, parts) in enumerate(shards):
        reps = LANES // depth
        starts.append(pl.multiple_of(row // reps * LANES, LANES))
        share = blocks // len(parts)
        for b in range(blocks):
            weights[b, s * 2 * LANES:(s + 1) * 2 * LANES, :] = place(
                parts[b // share], b % share, depth, row % reps
            )
    for t in range(tiles.shape[0]):
        left = jnp.concatenate(
            [tiles[t, p, :, pl.ds(start, LANES)] for start in starts for p in range(2)], axis=1
        )
        acc[slots[t]] += jnp.dot(left, weights[cols[t]], preferred_element_type=F32)


def hop_early(slots, cols, own, from_left, from_right, tiles, out, weights, *, n, depth):
    out[...] = jnp.zeros_like(out)
    shards = [
        (shard_row(n, 0), depth, [own]),
        (shard_row(n, -1), depth, [from_left]),
        (shard_row(n, 1), depth, [from_right]),
    ]
    accumulate(slots, cols, tiles, shards, out, weights)


def hop_middle(slots, cols, from_left, from_right, tiles, start, out, weights, *, n, depth, hop):
    del start
    shards = [
        (shard_row(n, -hop), depth, [from_left]), (shard_row(n, hop), depth, [from_right])
    ]
    accumulate(slots, cols, tiles, shards, out, weights)


def hop_last(slots, cols, pole_weight, low, high, tiles, start, out, dens, weights, *, n, depth):
    del start
    accumulate(slots, cols, tiles, [(shard_row(n, n // 2), depth, [low, high])], out, weights)
    width = dens.shape[2]
    for slot in range(out.shape[0]):
        dens[slot] = -(pole_weight[0] * out[slot, :, width:] + pole_weight[1] * out[slot, :, :width])


def halves_kernel(acc, mine, other):
    col = lax.axis_index("col")
    half = mine.shape[2]
    width = mine.shape[3]
    for slot in range(acc.shape[0]):
        for p in range(2):
            cut = slice(p * width, (p + 1) * width)
            mine[slot, p] = -acc[slot, pl.ds(pl.multiple_of(col * half, half), half), cut]
            other[slot, p] = -acc[slot, pl.ds(pl.multiple_of((1 - col) * half, half), half), cut]


def earlier(total):
    first = lax.broadcasted_iota(jnp.int32, (total, total), 0)
    second = lax.broadcasted_iota(jnp.int32, (total, total), 1)
    return (first < second).astype(F32).astype(BF16)


def peers(n):
    half = n // 2
    return list(range(half, n - 2)) + [n - 1], list(range(1, half)) + [n - 2]


def place_of(chip, n):
    apart = chip ^ lax.axis_index("row")
    place = jnp.zeros_like(apart)
    for core, steps in enumerate(peers(n)):
        first = jnp.where(lax.axis_index("col") == core, 1, 1 + n // 2)
        for step, k in enumerate(steps):
            place = jnp.where(apart == k, first + step, place)
    return place


def basis_kernel(wanted, basis, supernode, out, wide, *, n, rows_chip, slots):
    wide[...] = supernode[...].astype(F32)
    boxes, orbitals, _ = basis.shape
    total = boxes * orbitals
    rows = wanted[...]
    asked = jnp.concatenate([rows[b:b + 1] for b in range(boxes)], axis=1)
    source = asked // rows_chip
    marks = (lax.broadcasted_iota(jnp.int32, (n, total), 0) == source).astype(F32)
    counts = jnp.dot(marks.astype(BF16), earlier(total), preferred_element_type=F32)
    rank = jnp.sum(marks * counts, axis=0, keepdims=True).astype(jnp.int32)
    slot = place_of(source, n) * slots + rank
    index = lax.broadcasted_iota(jnp.int32, (out.shape[1], orbitals), 0)
    for b in range(boxes):
        pick = (index == slot[:, b * orbitals:(b + 1) * orbitals]).astype(F32).astype(BF16)
        out[b] = jnp.dot(pick, basis[b], preferred_element_type=F32).astype(BF16)


def lines_kernel(*refs, n, hops, lines):
    *shards, out = refs
    for ref, hop in zip(shards, hops):
        at = pl.multiple_of(shard_row(n, hop) * lines, lines)
        out[pl.ds(at, lines), :] = ref[ref.shape[0] - lines:, :]


def pick_kernel(mine, theirs, out, *, n, lines, total, rows_chip, slots):
    row = lax.axis_index("row")
    col = lax.axis_index("col")
    far, near = peers(n)
    far = far + near[-1:]

    def asked_by(chip, own):
        at = pl.ds(pl.multiple_of(chip * lines, lines), lines)
        return undigits(jnp.where(own, mine[at, :].astype(F32), theirs[at, :].astype(F32)), total)

    asked = [asked_by(row, True)]
    for step in range(n // 2):
        chip = row ^ jnp.where(col == 0, far[step], near[step])
        asked += [asked_by(chip, col == 0), asked_by(chip, col == 1)]
    count = len(asked)
    asked = jnp.concatenate(asked, axis=0).astype(jnp.int32)
    here = (asked // rows_chip) == row
    local = (asked % rows_chip).astype(F32)
    rank = jnp.dot(
        here.astype(F32).astype(BF16), earlier(total), preferred_element_type=F32
    ).astype(jnp.int32)
    rank = jnp.where(here, rank, -1)
    index = lax.broadcasted_iota(jnp.int32, (slots, total), 0)
    lane = lax.broadcasted_iota(jnp.int32, (slots, rows_chip), 1)
    for d in range(count):
        chosen = jnp.where(index == rank[d:d + 1], local[d:d + 1], 0.0)
        at = jnp.sum(chosen, axis=1, keepdims=True).astype(jnp.int32)
        out[d * slots:(d + 1) * slots, :] = (lane == at).astype(F32).astype(BF16)


def add_kernel(mine, theirs, out):
    out[...] = mine[...] + theirs[...]


def select_kernel(pick, mine, theirs, *outs):
    rows = pick.shape[1]
    total = (mine[...] + theirs[...]).reshape(rows, mine.shape[2]).astype(BF16)
    rows_out = jnp.dot(pick[...], total, preferred_element_type=F32).astype(BF16)
    at = 0
    for out in outs:
        out[...] = rows_out[at:at + out.shape[0]]
        at += out.shape[0]


def turn_kernel(*refs):
    *parts, out = refs
    slots = out.shape[0] // len(parts)
    at = pl.ds(pl.multiple_of((1 - lax.axis_index("col")) * slots, slots), slots)
    for i, part in enumerate(parts):
        out[i * slots:(i + 1) * slots] = part[at, :]


def first_kernel(*refs):
    own, *parts, basis, out = refs
    slots = own.shape[0]
    at = pl.ds(pl.multiple_of(lax.axis_index("col") * slots, slots), slots)
    arrived = jnp.concatenate([own[...]] + [part[at, :] for part in parts], axis=0)
    for n in range(basis.shape[0]):
        out[n] = lax.dot_general(
            arrived,
            basis[n, :arrived.shape[0], :],
            (((0,), (0,)), ((), ())),
            preferred_element_type=F32,
        )


def density_kernel(passed, first, basis, supernode, out):
    for n in range(basis.shape[0]):
        projected = first[n] + lax.dot_general(
            passed[...],
            basis[n, basis.shape[1] - passed.shape[0]:, :],
            (((0,), (0,)), ((), ())),
            preferred_element_type=F32,
        )
        out[n:n + 1, :] = jnp.sum(supernode[n] * projected, axis=0, keepdims=True)


def local(n_row, panel, tiles, tile_slot, tile_col, pole_weight, box_orbitals, box_basis, supernode_basis):
    order = ring_order(n_row)
    half_ring = n_row // 2
    to_right = [(order[i], order[(i + 1) % n_row]) for i in range(n_row)]
    to_left = [(order[(i + 1) % n_row], order[i]) for i in range(n_row)]
    _, blocks, parts, depth, width = panel.shape
    tile_count, _, order_b, _ = tiles.shape
    boxes, orbitals = box_orbitals.shape
    total = boxes * orbitals
    rows_chip = BR_DEV * order_b
    slots = 2 * total // n_row
    arrive = (1 + 2 * half_ring) * slots
    half = order_b // 2
    shard_rows = blocks * parts * depth
    lines = -(-2 * total // (16 * LANES)) * 16
    acc_shape = (BR_DEV, order_b, 2 * width)
    acc_out = jax.ShapeDtypeStruct(acc_shape, F32)
    in_vmem = pl.BlockSpec(memory_space=pltpu.VMEM)
    in_smem = pl.BlockSpec(memory_space=pltpu.SMEM)
    params = pltpu.CompilerParams(vmem_limit_bytes=VMEM_LIMIT)
    cost = pl.CostEstimate(flops=2 ** 20, bytes_accessed=2 ** 20, transcendentals=0)

    def call(body, in_specs, out_shape, before, shards, aliases={}):
        weights = pltpu.VMEM((blocks, shards * 2 * LANES, 2 * width), BF16)
        return pl.pallas_call(
            functools.partial(body, n=n_row, depth=depth),
            in_specs=in_specs,
            out_specs=jax.tree.map(lambda _: in_vmem, out_shape),
            out_shape=out_shape,
            scratch_shapes=[*before, weights],
            input_output_aliases=aliases,
            compiler_params=params,
            cost_estimate=cost,
        )

    own = panel.reshape(shard_rows, width)
    own_lines = pl.pallas_call(
        digits_kernel,
        out_shape=jax.ShapeDtypeStruct((lines, width), BF16),
        compiler_params=params,
        cost_estimate=pl.CostEstimate(flops=2 ** 34, bytes_accessed=2 ** 10, transcendentals=0),
    )(box_orbitals)
    pack = pl.pallas_call(
        pack_kernel,
        out_shape=jax.ShapeDtypeStruct((shard_rows + lines, width), BF16),
        compiler_params=params,
        cost_estimate=cost,
    )

    basis_here, wide = pl.pallas_call(
        functools.partial(basis_kernel, n=n_row, rows_chip=rows_chip, slots=slots),
        out_shape=[
            jax.ShapeDtypeStruct((boxes, arrive, box_basis.shape[2]), BF16),
            jax.ShapeDtypeStruct(supernode_basis.shape, F32),
        ],
        compiler_params=params,
        cost_estimate=cost,
    )(box_orbitals, box_basis, supernode_basis)

    left, right = own, own
    seen, hops = [own_lines], [0]
    acc = None
    for h in range(1, half_ring + 1):
        if h < half_ring:
            next_left = lax.ppermute(left, "row", to_right)
            next_right = lax.ppermute(right, "row", to_left)
        else:
            cut = shard_rows // 2
            next_left = lax.ppermute(left[:cut], "row", to_right)
            next_right = lax.ppermute(right[cut:], "row", to_left)
        if h == 1:
            seen += [
                lax.ppermute(own_lines, "row", to_right), lax.ppermute(own_lines, "row", to_left)
            ]
            hops += [-1, 1]
            left, right = pack(next_left, seen[1]), pack(next_right, seen[2])
            continue
        if h == 2:
            acc = call(hop_early, [in_smem] * 2 + [in_vmem] * 4, acc_out, [], 3)(
                tile_slot, tile_col, own, left, right, tiles
            )
        elif h > 2:
            acc = call(
                functools.partial(hop_middle, hop=h - 1),
                [in_smem] * 2 + [in_vmem] * 4,
                acc_out,
                [],
                2,
                aliases={5: 0},
            )(tile_slot, tile_col, left, right, tiles, acc)
        left, done = lax.optimization_barrier((next_left, acc))
        right, _ = lax.optimization_barrier((next_right, acc))
        acc = done
        if h < half_ring:
            seen += [left, right]
            hops += [-h, h]
        else:
            seen.append(right)
            hops.append(h)

    swap = [(0, 1), (1, 0)]
    wanted = pl.pallas_call(
        functools.partial(lines_kernel, n=n_row, hops=hops, lines=lines),
        out_shape=jax.ShapeDtypeStruct((n_row * lines, width), BF16),
        compiler_params=params,
        cost_estimate=cost,
    )(*seen)
    left, wanted, basis_here, wide = lax.optimization_barrier((left, wanted, basis_here, wide))
    wanted_other = lax.ppermute(wanted, "col", swap)

    half_shape = (BR_DEV, 2, half, width)
    acc, dens = call(
        hop_last,
        [in_smem] * 3 + [in_vmem] * 4,
        [acc_out, jax.ShapeDtypeStruct((BR_DEV, order_b, width), F32)],
        [],
        1,
        aliases={6: 0},
    )(tile_slot, tile_col, pole_weight, left, right, tiles, acc)
    dens, wanted_other = lax.optimization_barrier((dens, wanted_other))
    dens_other = lax.ppermute(dens, "col", swap)
    pick = pl.pallas_call(
        functools.partial(
            pick_kernel, n=n_row, lines=lines, total=total, rows_chip=rows_chip, slots=slots
        ),
        out_shape=jax.ShapeDtypeStruct((arrive, rows_chip), BF16),
        compiler_params=params,
        cost_estimate=pl.CostEstimate(flops=2 ** 32, bytes_accessed=2 ** 20, transcendentals=0),
    )(wanted, wanted_other)
    message = jax.ShapeDtypeStruct((2 * slots, width), BF16)
    kept, *sent = pl.pallas_call(
        select_kernel,
        out_shape=[jax.ShapeDtypeStruct((slots, width), BF16)] + [message] * half_ring,
        compiler_params=params,
        cost_estimate=cost,
    )(pick, dens, dens_other)

    far, near = peers(n_row)
    fetched = []
    for step in range(half_ring):
        pairs = [(2 * r + 1, 2 * (r ^ near[step]) + 1) for r in range(n_row)]
        if step < len(far):
            pairs += [(2 * r, 2 * (r ^ far[step])) for r in range(n_row)]
        fetched.append(lax.ppermute(sent[step], ("row", "col"), pairs))

    mine, other = pl.pallas_call(
        halves_kernel,
        out_shape=[jax.ShapeDtypeStruct(half_shape, F32)] * 2,
        compiler_params=params,
        cost_estimate=cost,
    )(acc)
    inverse_other = lax.ppermute(other, "col", swap)
    inverse = pl.pallas_call(
        add_kernel,
        out_shape=jax.ShapeDtypeStruct(half_shape, F32),
        compiler_params=params,
        cost_estimate=cost,
    )(mine, inverse_other)
    fetched[0], inverse = lax.optimization_barrier((fetched[0], inverse))
    turned = pl.pallas_call(
        turn_kernel,
        out_shape=jax.ShapeDtypeStruct((half_ring * slots, width), BF16),
        compiler_params=params,
        cost_estimate=cost,
    )(*fetched)
    passed = lax.ppermute(turned, "col", swap)
    first = pl.pallas_call(
        first_kernel,
        out_shape=jax.ShapeDtypeStruct((boxes, width, box_basis.shape[2]), F32),
        compiler_params=params,
        cost_estimate=cost,
    )(kept, *fetched, basis_here)
    density = pl.pallas_call(
        density_kernel,
        out_shape=jax.ShapeDtypeStruct((boxes, box_basis.shape[2]), F32),
        compiler_params=params,
    )(passed, first, basis_here, wide)
    return inverse, density


def solution(mesh):
    return jax.shard_map(
        functools.partial(local, mesh.shape["row"]),
        mesh=mesh,
        in_specs=(
            P(("pole", "col"), None, None, "row", None),
            P(("pole", "row", "col"), None, None, None),
            P(("pole", "row", "col")),
            P(("pole", "row", "col")),
            P("pole"),
            P(("pole", "row", "col"), None),
            P(("pole", "row", "col"), None, None),
            P(("pole", "row", "col"), None, None),
        ),
        out_specs=(P(("pole", "row"), None, "col", None), P(("pole", "row", "col"), None)),
        check_vma=False,
    )
```
